32 devices in a mesh: members: 2 (over y), sub: 4 (over z), lev: 4 (over x, core).
Axes of the slice: x: 2, y: 2, z: 4, core: 2. Of those that a mesh axis runs over, the one named last changes fastest.
Arguments:
- tracer: float32 [96, 32, 512], P(('members', 'lev'), None, 'sub'), parts along dimension 0, may hold values from -6 to 6
- zonal_flow: float32 [96, 32, 512], P(('members', 'lev'), None, 'sub'), parts along dimension 0, may hold values from -1 to 1
- meridional_flow: float32 [96, 32, 512], P(('members', 'lev'), None, 'sub'), parts along dimension 0, may hold values from -1 to 1
- cotangent: float32 [96, 32, 512], P(('members', 'lev'), None, 'sub'), parts along dimension 0, may hold values from -6 to 6
- thickness: float32 [48], replicated, may hold values from 0.5 to 2
- wet_levels: int32 [32, 512], P(None, 'sub'), may hold values from 0 to 48
Outputs:
- next_tracer: float32 [96, 32, 512], P(('members', 'lev'), None, 'sub'), parts along dimension 0
- tracer_adjoint: float32 [96, 32, 512], P(('members', 'lev'), None, 'sub'), parts along dimension 0
- surface_adjoint: float32 [64, 512], P('members', 'sub'), parts along dimension 0
The draws below stay inside these ranges and needn't reach their ends.
There are 2 independent parts, one for each index of `members`. The reference program is written for one: setup_inputs(seed, part) draws one part's arguments, and reference() takes and returns one part's arrays. A program takes and returns all parts, laid end to end along the dimension named above; an argument that names none is the same for every part. Nothing has to cross between parts.
Inputs may be any that keep to these rules, and one draw needn't show every extreme that they name: Level k (counted from 0) of a column is wet when k < wet_levels, land otherwise; 0 marks a land column.
All inputs are finite; a program needn't handle non-finite values.
Results may differ from the reference program's by a relative error of at most 0.0001.
Values sent between devices are 32-bit elements; how exact they have to be, the bound alone decides.
No kernel may reach another device: no remote copies, remote signals or barrier semaphores. Data moves between devices by JAX's collectives and lax.ppermute only.
A program may use at most 64 MiB of HBM per device.

```python
import math
import jax
import jax.numpy as jnp
from jax import lax

NY = 32
ITERS = 3
NZ = 48
NX = 512


def with_ends(array, key, smallest, largest):
    shape = array.shape
    place = [jax.random.randint(jax.random.fold_in(key, axis), (), 0, shape[axis]) for axis in range(len(shape))]
    array = array.at[tuple(place)].set(smallest)
    longest = shape.index(max(shape))
    place[longest] = (place[longest] + 1) % shape[longest]
    return array.at[tuple(place)].set(largest)


def block_scale(own_key, dims, pieces, least, high):
    def one(position, blocks):
        steps = jax.random.uniform(jax.random.fold_in(jax.random.fold_in(own_key, 6), position), (blocks,), jnp.float32, least / len(pieces), high / len(pieces))
        return jnp.repeat(jnp.exp(steps), dims[position] // blocks).reshape((-1,) + (1,) * (len(dims) - position - 1))

    level = one(*pieces[0])
    for cut in pieces[1:]:
        level = level * one(*cut)
    return level


def bell_draw(stream_key, shape, width, most, split=(), held_as=jnp.bfloat16):
    gain = block_scale(stream_key, shape, split, -0.22, 0.18) if split else 1.0
    entries = jax.random.normal(stream_key, shape, jnp.float32) * width * gain
    return jnp.minimum(jnp.maximum(entries, -most), most).astype(held_as)


def setup_inputs(seed: int = 0, part: int = 0) -> dict:
    key_of = jax.random.split(jax.random.key(seed), 7)
    part_splits = jax.random.split(jax.random.fold_in(key_of[6], part), 7)
    return {
        "tracer": bell_draw(part_splits[0], (NZ, NY, NX), 1.0, 6.0, ((0, 4), (2, 4)), jnp.float32),
        "zonal_flow": jnp.clip(jax.random.uniform(part_splits[1], (NZ, NY, NX), jnp.float32, -1.0, 1.0) * block_scale(part_splits[1], (NZ, NY, NX), ((0, 4), (2, 4)), -0.4, 0.0), -1.0, 1.0),
        "meridional_flow": jnp.clip(jax.random.uniform(part_splits[2], (NZ, NY, NX), jnp.float32, -1.0, 1.0) * block_scale(part_splits[2], (NZ, NY, NX), ((0, 4), (2, 4)), -0.4, 0.0), -1.0, 1.0),
        "cotangent": bell_draw(part_splits[3], (NZ, NY, NX), 1.0, 6.0, ((0, 4), (2, 4)), jnp.float32),
        "thickness": jnp.clip(jnp.exp(jax.random.uniform(key_of[4], (NZ,), jnp.float32, math.log(0.5), math.log(2.0))), 0.5, 2.0),
        "wet_levels": with_ends(jax.random.randint(key_of[5], (NY, NX), 0, NZ + 1), jax.random.fold_in(key_of[5], 1), 0, NZ).astype(jnp.int32),
    }


ADVECT_STEP = 0.25
MIX_RATE = 2.0

def advect(values, zonal_flow, meridional_flow, wet_mask):
    flux_x = zonal_flow * (jnp.roll(values, 1, axis=2) + values) * 0.5
    flux_y = meridional_flow * (jnp.roll(values, 1, axis=1) + values) * 0.5
    change = jnp.roll(flux_x, -1, axis=2) - flux_x + (jnp.roll(flux_y, -1, axis=1) - flux_y)
    return wet_mask * (values - ADVECT_STEP * change)

def thomas(lower_band, diagonal, upper_band, right_side):
    count = len(diagonal)
    ratios = []
    partial_value = []
    divisor = diagonal[0]
    ratios.append(upper_band[0] / divisor)
    partial_value.append(right_side[0] / divisor)
    for k in range(1, count):
        divisor = diagonal[k] - lower_band[k] * ratios[k - 1]
        ratios.append(upper_band[k] / divisor)
        partial_value.append((right_side[k] - lower_band[k] * partial_value[k - 1]) / divisor)
    result_rows = [None] * count
    result_rows[count - 1] = partial_value[count - 1]
    for k in range(count - 2, -1, -1):
        result_rows[k] = partial_value[k] - ratios[k] * result_rows[k + 1]
    return jnp.stack(result_rows)

def mix_columns(forward, cotangent, thickness, wet_mask):
    count = forward.shape[0]
    empty_level = jnp.zeros_like(forward[0])
    conduct = [empty_level]
    for k in range(1, count):
        spacing = 0.5 * (thickness[k - 1] + thickness[k])
        gradient = (forward[k] - forward[k - 1]) / spacing
        conduct.append(MIX_RATE * wet_mask[k] * (0.2 + 1.0 / (1.0 + gradient * gradient)) / spacing)
    conduct.append(empty_level)
    diagonal = [1.0 + (conduct[k] + conduct[k + 1]) / thickness[k] for k in range(count)]
    lower_band = [-conduct[k] / thickness[k] for k in range(count)]
    upper_band = [-conduct[k + 1] / thickness[k] for k in range(count)]
    lower_trans = [empty_level] + [-conduct[k] / thickness[k - 1] for k in range(1, count)]
    upper_trans = [-conduct[k + 1] / thickness[k + 1] for k in range(count - 1)] + [empty_level]
    mixed = thomas(lower_band, diagonal, upper_band, [forward[k] for k in range(count)])
    adjoint = thomas(lower_trans, diagonal, upper_trans, [cotangent[k] for k in range(count)])
    return (mixed, adjoint)

def barotropic(surface_field, damping):
    beside = jnp.roll(surface_field, 1, axis=1) + jnp.roll(surface_field, -1, axis=1)
    beside = beside + jnp.roll(surface_field, 1, axis=0) + jnp.roll(surface_field, -1, axis=0)
    return (4.0 + damping) * surface_field - beside

def reference(tracer, zonal_flow, meridional_flow, cotangent, thickness, wet_levels):
    levels = jnp.arange(NZ, dtype=jnp.int32).reshape(NZ, 1, 1)
    wet_mask = (levels < wet_levels[None]).astype(jnp.float32)
    forward = advect(tracer, zonal_flow, meridional_flow, wet_mask)
    next_tracer, mixed_adjoint = mix_columns(forward, cotangent, thickness, wet_mask)
    _, pullback = jax.vjp(lambda values: advect(values, zonal_flow, meridional_flow, wet_mask), tracer)
    tracer_adjoint = pullback(mixed_adjoint)[0]
    column = thickness.reshape(NZ, 1, 1)
    source = lax.optimization_barrier(jnp.sum(column * mixed_adjoint, axis=0))
    damping = 0.3 + lax.optimization_barrier(jnp.sum(column * wet_mask, axis=0)) / NZ
    surface = jnp.zeros_like(source)
    residual = source
    direction = source
    norm_now = jnp.sum(residual * residual)
    for sweep in range(ITERS):
        image_field = barotropic(direction, damping)
        step_size = norm_now / jnp.sum(direction * image_field)
        surface = surface + step_size * direction
        residual = residual - step_size * image_field
        norm_next = jnp.sum(residual * residual)
        direction = residual + norm_next / norm_now * direction
        norm_now = norm_next
    return (next_tracer, tracer_adjoint, surface)
```

```python
import functools

import jax
import jax.numpy as jnp
from jax import lax
from jax.experimental import pallas as pl
from jax.experimental.pallas import tpu as pltpu
from jax.sharding import PartitionSpec as P

ITERS = 3
ADVECT_STEP = 0.25
MIX_RATE = 2.0
HALF_STEP = 0.5 * ADVECT_STEP

N_BLOCK = 12
N_LAST = 6

VMEM_IN = pl.BlockSpec(memory_space=pltpu.VMEM)
SMEM_IN = pl.BlockSpec(memory_space=pltpu.SMEM)


def in_vmem(*shape):
    return pltpu.VMEM(shape, jnp.float32)


def lanes(rows, width):
    return lax.broadcasted_iota(jnp.int32, (rows, width), 1)


def turn(field, shift, axis):
    size = field.shape[axis]
    shift = shift % size
    return field if shift == 0 else pltpu.roll(field, shift, axis)


def splat(scalar, width):
    return jnp.full((1, width), scalar, jnp.float32)


def conductance(drop, upper_thick, lower_thick, wet):
    spacing = 0.5 * (upper_thick + lower_thick)
    rate = 0.2 / spacing + spacing / (spacing * spacing + drop * drop)
    return jnp.where(wet, MIX_RATE * rate, 0.0)


def pack_kernel(tracer_ref, zonal_ref, east_ref, west_ref):
    own, rows, width = tracer_ref.shape
    lane = lanes(rows, width)
    east = jnp.zeros((rows, width), jnp.float32)
    west = jnp.zeros((rows, width), jnp.float32)
    for k in range(own):
        values = tracer_ref[k]
        east = jnp.where(lane == k, turn(values, k + 1, 1), east)
        west = jnp.where(lane == k, turn(values, k, 1), west)
        west = jnp.where(lane == own + k, turn(zonal_ref[k], own + k, 1), west)
    east_ref[...] = east
    west_ref[...] = west


def local_kernel(
    thick_ref, wet_ref, tracer_ref, zonal_ref, merid_ref, cot_ref, from_west_ref, from_east_ref,
    block_ref, forward_ref, adjoint_ref, top_ref, bottom_ref, u_next_ref, damping_ref,
):
    own, rows, width = tracer_ref.shape
    level_count = thick_ref.shape[0]
    first = lax.axis_index("lev") * own
    lane = lanes(rows, width)
    wet_levels = wet_ref[...]
    from_west = from_west_ref[...]
    from_east = from_east_ref[...]
    forward = []
    for k in range(own):
        values = tracer_ref[k]
        zonal = zonal_ref[k]
        merid = merid_ref[k]
        c_west = jnp.where(lane == 0, turn(from_west, -k, 1), turn(values, 1, 1))
        c_east = jnp.where(lane == width - 1, turn(from_east, width - 1 - k, 1), turn(values, -1, 1))
        u_next = jnp.where(lane == width - 1, turn(from_east, width - 1 - own - k, 1), turn(zonal, -1, 1))
        u_next_ref[k] = u_next
        flux_y = merid * (turn(values, 1, 0) + values)
        change = u_next * (values + c_east) - zonal * (c_west + values) + (turn(flux_y, -1, 0) - flux_y)
        forward.append(jnp.where(wet_levels > first + k, values - HALF_STEP * change, 0.0))

    thick = [splat(thick_ref[first + k], width) for k in range(own)]
    conduct = [None]
    for k in range(1, own):
        conduct.append(
            conductance(forward[k] - forward[k - 1], thick[k - 1], thick[k], wet_levels > first + k)
        )
    pivot = jnp.broadcast_to(thick[0], (rows, width))
    ratio, scale = [None], []
    g_forward = [thick[0] * forward[0]]
    g_adjoint = [cot_ref[0]]
    g_top = [jnp.ones((rows, width), jnp.float32)]
    for k in range(1, own):
        inverse = 1.0 / (pivot + conduct[k])
        scale.append(inverse)
        ratio.append(conduct[k] * inverse)
        pivot = thick[k] + pivot * ratio[k]
        g_forward.append(thick[k] * forward[k] + ratio[k] * g_forward[k - 1])
        g_adjoint.append(cot_ref[k] + ratio[k] * g_adjoint[k - 1])
        g_top.append(ratio[k] * g_top[k - 1])
    scale.append(1.0 / pivot)
    last = own - 1
    y_forward = g_forward[last] * scale[last]
    y_adjoint = g_adjoint[last] * scale[last]
    y_top = g_top[last] * scale[last]
    y_bottom = scale[last]
    block_ref[1] = y_top
    block_ref[2] = y_bottom
    block_ref[4] = y_forward
    block_ref[6] = y_adjoint
    block_ref[7] = forward[0]
    block_ref[8] = forward[last]
    sums = [jnp.zeros((rows, width), jnp.float32)] * 3
    for k in range(last, -1, -1):
        if k < last:
            y_forward = g_forward[k] * scale[k] + ratio[k + 1] * y_forward
            y_adjoint = g_adjoint[k] * scale[k] + ratio[k + 1] * y_adjoint
            y_top = g_top[k] * scale[k] + ratio[k + 1] * y_top
            y_bottom = ratio[k + 1] * y_bottom
        forward_ref[k] = y_forward
        adjoint_ref[k] = y_adjoint
        top_ref[k] = y_top
        bottom_ref[k] = y_bottom
        square = thick[k] * thick[k]
        sums = [s + square * y for s, y in zip(sums, (y_adjoint, y_top, y_bottom))]
    block_ref[0] = y_top
    block_ref[3] = y_forward
    block_ref[5] = y_adjoint
    block_ref[9] = sums[0]
    block_ref[10] = sums[1]
    block_ref[11] = sums[2]

    def add_level(k, total):
        return total + jnp.where(wet_levels > k, thick_ref[k], 0.0)

    depth = lax.fori_loop(0, level_count, add_level, jnp.zeros((rows, width), jnp.float32), unroll=8)
    damping_ref[...] = 0.3 + depth / level_count


def merge_kernel(size, final, own, thick_ref, wet_ref, mine_ref, other_ref, block_ref, flux_ref):
    place = lax.axis_index("lev")
    width = wet_ref.shape[1]
    upper = lax.rem(place // size, 2) == 0
    above = [jnp.where(upper, mine_ref[i], other_ref[i]) for i in range(N_BLOCK)]
    below = [jnp.where(upper, other_ref[i], mine_ref[i]) for i in range(N_BLOCK)]
    start = (place // (2 * size) * 2 + 1) * size * own
    rate = conductance(
        below[7] - above[8],
        splat(thick_ref[start - 1], width),
        splat(thick_ref[start], width),
        wet_ref[...] > start,
    )
    rate = rate / (1.0 + rate * (below[0] + above[2]))
    by_forward = rate * (below[3] - above[4])
    by_adjoint = rate * (below[5] - above[6])
    by_top = -rate * above[1]
    by_bottom = rate * below[1]
    flux_ref[0] = by_forward
    flux_ref[1] = by_adjoint
    flux_ref[2] = by_top
    flux_ref[3] = by_bottom
    spread = above[11] - below[10]
    merged = [
        above[0] + above[1] * by_top,
        -below[1] * by_top,
        below[2] - below[1] * by_bottom,
        above[3] + above[1] * by_forward,
        below[4] - below[1] * by_forward,
        above[5] + above[1] * by_adjoint,
        below[6] - below[1] * by_adjoint,
        above[7],
        below[8],
        above[9] + below[9] + by_adjoint * spread,
        above[10] + by_top * spread,
        below[11] + by_bottom * spread,
    ]
    if final:
        upper_next = lax.rem(place // (2 * size), 2) == 0
        merged = last_fields(upper_next, merged)
    for i, field in enumerate(merged):
        block_ref[i] = field


def last_fields(upper, block):
    return [
        jnp.where(upper, block[2], block[0]),
        jnp.where(upper, block[4], block[3]),
        jnp.where(upper, block[6], block[5]),
        jnp.where(upper, block[8], block[7]),
        block[9],
        jnp.where(upper, block[11], block[10]),
    ]


def pick_kernel(size, block_ref, out_ref):
    upper = lax.rem(lax.axis_index("lev") // size, 2) == 0
    block = [block_ref[i] for i in range(N_BLOCK)]
    for i, field in enumerate(last_fields(upper, block)):
        out_ref[i] = field


def final_kernel(
    sizes, own, thick_ref, wet_ref, mine_ref, other_ref, adjoint_ref, top_ref, bottom_ref, damping_ref, *rest
):
    flux_refs, message_ref, ends_ref, pulled_ref = rest[:-3], rest[-3], rest[-2], rest[-1]
    rows, width = wet_ref.shape
    place = lax.axis_index("lev")
    size = sizes[-1]
    upper = lax.rem(place // size, 2) == 0
    start = (place // (2 * size) * 2 + 1) * size * own
    wet_levels = wet_ref[...]
    rate = conductance(
        mine_ref[3] - other_ref[3],
        splat(thick_ref[start - 1], width),
        splat(thick_ref[start], width),
        wet_levels > start,
    )
    rate = rate / (1.0 + rate * (mine_ref[0] + other_ref[0]))
    in_forward = rate * (other_ref[1] - mine_ref[1])
    in_adjoint = rate * (other_ref[2] - mine_ref[2])
    source = mine_ref[4] + other_ref[4] + in_adjoint * (mine_ref[5] - other_ref[5])
    ends = []
    for into, index in ((in_forward, 0), (in_adjoint, 1)):
        top = jnp.where(upper, 0.0, into)
        bottom = jnp.where(upper, into, 0.0)
        for step in range(len(sizes) - 2, -1, -1):
            flux_ref = flux_refs[step]
            flux = flux_ref[index] + top * flux_ref[2] + bottom * flux_ref[3]
            above = lax.rem(place // sizes[step], 2) == 0
            top, bottom = jnp.where(above, top, -flux), jnp.where(above, flux, bottom)
        ends += [top, bottom]
    for i in range(4):
        ends_ref[i] = ends[i]
    lane = lanes(rows, width)
    first = place * own
    edges = jnp.zeros((rows, width), jnp.float32)
    for k in range(own):
        mixed = adjoint_ref[k] + top_ref[k] * ends[2] + bottom_ref[k] * ends[3]
        pulled = jnp.where(wet_levels > first + k, thick_ref[first + k] * mixed, 0.0)
        pulled_ref[k] = pulled
        edges = jnp.where(lane == k, turn(pulled, k, 1), edges)
        edges = jnp.where(lane == own + k, turn(pulled, own + k + 1, 1), edges)
    message_ref[0] = source
    message_ref[1] = edges
    message_ref[2] = damping_ref[...]


def forward_kernel(forward_ref, top_ref, bottom_ref, ends_ref, out_ref):
    top = ends_ref[0]
    bottom = ends_ref[1]
    for k in range(forward_ref.shape[0]):
        out_ref[k] = forward_ref[k] + top_ref[k] * top + bottom_ref[k] * bottom


def total(field):
    while field.ndim > 2:
        field = jnp.sum(field, axis=0)
    return jnp.sum(jnp.sum(field, axis=0, keepdims=True), axis=1, keepdims=True)


def surface_kernel(
    pulled_ref, zonal_ref, merid_ref, u_next_ref, messages_ref, tracer_adjoint_ref, surface_ref,
    source_scr, damping_scr,
):
    own, rows, width = pulled_ref.shape
    count = messages_ref.shape[0]
    place = lax.axis_index("sub")
    lane = lanes(rows, width)
    west_edges = jnp.zeros((rows, width), jnp.float32)
    east_edges = jnp.zeros((rows, width), jnp.float32)
    for i in range(count):
        owner = jnp.bitwise_xor(place, i)
        source_scr[owner] = messages_ref[i, 0]
        damping_scr[owner] = messages_ref[i, 2]
    west_edges = messages_ref[jnp.bitwise_xor(place, lax.rem(place + count - 1, count)), 1]
    east_edges = messages_ref[jnp.bitwise_xor(place, lax.rem(place + 1, count)), 1]
    for k in range(own):
        pulled = pulled_ref[k]
        merid = merid_ref[k]
        b_west = jnp.where(lane == 0, turn(west_edges, -own - k, 1), turn(pulled, 1, 1))
        b_east = jnp.where(lane == width - 1, turn(east_edges, width - 1 - k, 1), turn(pulled, -1, 1))
        across = zonal_ref[k] * (pulled - b_west) + u_next_ref[k] * (b_east - pulled)
        step = merid * (pulled - turn(pulled, 1, 0))
        across = across + step + turn(step, -1, 0)
        tracer_adjoint_ref[k] = pulled + HALF_STEP * across

    first_lane = lax.broadcasted_iota(jnp.int32, (count, rows, width), 2) == 0
    last_lane = lax.broadcasted_iota(jnp.int32, (count, rows, width), 2) == width - 1
    damping = 4.0 + damping_scr[...]

    def beside(field, shift):
        return jnp.concatenate([field[-shift:], field[:-shift]]) if count > 1 else field

    def image_of(field):
        west = turn(field, 1, 2)
        west = jnp.where(first_lane, beside(west, 1), west)
        east = turn(field, -1, 2)
        east = jnp.where(last_lane, beside(east, -1), east)
        return damping * field - (west + east + turn(field, 1, 1) + turn(field, -1, 1))

    residual = source_scr[...]
    image = image_of(residual)
    norm = total(residual * residual)
    step_size = norm / total(residual * image)
    direction, along = residual, image
    surface = jnp.zeros_like(residual)
    for sweep in range(ITERS):
        surface = surface + step_size * direction
        if sweep + 1 < ITERS:
            residual = residual - step_size * along
            image = image_of(residual)
            norm_next = total(residual * residual)
            product = total(residual * image)
            growth = norm_next / norm
            step_size = norm_next / (product - growth * norm_next / step_size)
            direction = residual + growth * direction
            along = image + growth * along
            norm = norm_next
    source_scr[...] = surface
    surface_ref[...] = source_scr[place]


def on_device(tracer, zonal_flow, meridional_flow, cotangent, thickness, wet_levels):
    own, rows, width = tracer.shape
    lev_count = lax.axis_size("lev")
    sub_count = lax.axis_size("sub")
    edge = in_vmem(rows, width)
    levels = in_vmem(own, rows, width)

    east, west = pl.pallas_call(
        pack_kernel, out_shape=(edge, edge), in_specs=[VMEM_IN] * 2, out_specs=(VMEM_IN,) * 2, name="pack"
    )(tracer, zonal_flow)
    ring = [(i, (i + 1) % sub_count) for i in range(sub_count)]
    from_west = lax.ppermute(east, "sub", ring)
    from_east = lax.ppermute(west, "sub", [(b, a) for a, b in ring])

    block, forward, adjoint, top, bottom, u_next, damping = pl.pallas_call(
        local_kernel,
        out_shape=(in_vmem(N_BLOCK, rows, width), levels, levels, levels, levels, levels, edge),
        in_specs=[SMEM_IN] + [VMEM_IN] * 7,
        out_specs=(VMEM_IN,) * 7,
        name="local",
    )(thickness, wet_levels, tracer, zonal_flow, meridional_flow, cotangent, from_west, from_east)

    sizes = [1]
    while sizes[-1] * 2 < lev_count:
        sizes.append(sizes[-1] * 2)
    fluxes = []
    if len(sizes) == 1:
        block = pl.pallas_call(
            functools.partial(pick_kernel, 1), out_shape=in_vmem(N_LAST, rows, width),
            in_specs=[VMEM_IN], out_specs=VMEM_IN, name="pick",
        )(block)
    for size in sizes:
        other = lax.ppermute(block, "lev", [(i, i ^ size) for i in range(lev_count)])
        if size == sizes[-1]:
            break
        final = size * 2 == sizes[-1]
        block, flux = pl.pallas_call(
            functools.partial(merge_kernel, size, final, own),
            out_shape=(in_vmem(N_LAST if final else N_BLOCK, rows, width), in_vmem(4, rows, width)),
            in_specs=[SMEM_IN] + [VMEM_IN] * 3,
            out_specs=(VMEM_IN,) * 2,
            name="merge",
        )(thickness, wet_levels, block, other)
        fluxes.append(flux)

    message, ends, pulled = pl.pallas_call(
        functools.partial(final_kernel, sizes, own),
        out_shape=(in_vmem(3, rows, width), in_vmem(4, rows, width), levels),
        in_specs=[SMEM_IN] + [VMEM_IN] * (7 + len(fluxes)),
        out_specs=(VMEM_IN,) * 3,
        name="final",
    )(thickness, wet_levels, block, other, adjoint, top, bottom, damping, *fluxes)

    messages = message[None]
    size = 1
    while size < sub_count:
        got = lax.ppermute(messages, "sub", [(i, i ^ size) for i in range(sub_count)])
        messages = jnp.concatenate([messages, got])
        size *= 2

    next_tracer = pl.pallas_call(
        forward_kernel,
        out_shape=jax.ShapeDtypeStruct(tracer.shape, jnp.float32),
        in_specs=[VMEM_IN] * 4,
        out_specs=VMEM_IN,
        name="forward",
    )(forward, top, bottom, ends)

    tracer_adjoint, surface = pl.pallas_call(
        surface_kernel,
        out_shape=(
            jax.ShapeDtypeStruct(tracer.shape, jnp.float32),
            jax.ShapeDtypeStruct((rows, width), jnp.float32),
        ),
        in_specs=[VMEM_IN] * 5,
        out_specs=(VMEM_IN,) * 2,
        scratch_shapes=[pltpu.VMEM((sub_count, rows, width), jnp.float32)] * 2,
        name="surface",
    )(pulled, zonal_flow, meridional_flow, u_next, messages)
    return (next_tracer, tracer_adjoint, surface)


def solution(mesh):
    whole = P(("members", "lev"), None, "sub")
    return jax.shard_map(
        on_device,
        mesh=mesh,
        in_specs=(whole, whole, whole, whole, P(), P(None, "sub")),
        out_specs=(whole, whole, P("members", "sub")),
        check_vma=False,
    )
```

```python
import functools

import jax
import jax.numpy as jnp
from jax import lax
from jax.experimental import pallas as pl
from jax.experimental.pallas import tpu as pltpu
from jax.sharding import PartitionSpec as P

ITERS = 3
ADVECT_STEP = 0.25
MIX_RATE = 2.0
HALF_STEP = 0.5 * ADVECT_STEP

N_BLOCK = 12
N_LAST = 6

VMEM_IN = pl.BlockSpec(memory_space=pltpu.VMEM)
SMEM_IN = pl.BlockSpec(memory_space=pltpu.SMEM)


def in_vmem(*shape):
    return pltpu.VMEM(shape, jnp.float32)


def near(*arrays):
    return [pltpu.with_memory_space_constraint(array, pltpu.VMEM) for array in arrays]


def lanes(rows, width):
    return lax.broadcasted_iota(jnp.int32, (rows, width), 1)


def turn(field, shift, axis):
    size = field.shape[axis]
    shift = shift % size
    return field if shift == 0 else pltpu.roll(field, shift, axis)


def splat(scalar, width):
    return jnp.full((1, width), scalar, jnp.float32)


def conductance(drop, upper_thick, lower_thick, wet):
    spacing = 0.5 * (upper_thick + lower_thick)
    rate = 0.2 / spacing + spacing / (spacing * spacing + drop * drop)
    return jnp.where(wet, MIX_RATE * rate, 0.0)


def fold(field):
    rows, width = field.shape
    groups = rows // 8
    slot = width // groups
    lane = lanes(8, width)
    folded = field[:8]
    for group in range(1, groups):
        folded = jnp.where(lane // slot == group, turn(field[8 * group : 8 * group + 8], slot * group, 1), folded)
    return folded


def unfold(folded, rows):
    width = folded.shape[1]
    groups = rows // 8
    return jnp.concatenate([turn(folded, -(width // groups) * group, 1) for group in range(groups)])


def pack_kernel(tracer_hbm, zonal_hbm, wet_hbm, tracer_ref, zonal_ref, wet_ref, east_ref, west_ref, sems):
    own, rows, width = tracer_ref.shape
    copies = [
        pltpu.make_async_copy(source, target, sems.at[i])
        for i, (source, target) in enumerate(
            ((tracer_hbm, tracer_ref), (zonal_hbm, zonal_ref), (wet_hbm, wet_ref))
        )
    ]
    for copy in copies:
        copy.start()
    lane = lanes(rows, width)
    east = jnp.zeros((rows, width), jnp.float32)
    west = jnp.zeros((rows, width), jnp.float32)
    copies[0].wait()
    for k in range(own):
        values = tracer_ref[k]
        east = jnp.where(lane == k, turn(values, k + 1, 1), east)
        west = jnp.where(lane == k, turn(values, k, 1), west)
    east_ref[...] = fold(east)
    copies[1].wait()
    for k in range(own):
        west = jnp.where(lane == own + k, turn(zonal_ref[k], own + k, 1), west)
    west_ref[...] = fold(west)
    copies[2].wait()


def local_kernel(
    thick_ref, wet_ref, tracer_ref, zonal_ref, merid_ref, cot_ref, from_west_ref, from_east_ref,
    block_ref, forward_ref, adjoint_ref, top_ref, bottom_ref, u_next_ref, damping_ref,
):
    own, rows, width = tracer_ref.shape
    level_count = thick_ref.shape[0]
    first = lax.axis_index("lev") * own
    lane = lanes(rows, width)
    wet_levels = wet_ref[...]
    from_west = unfold(from_west_ref[...], rows)
    from_east = unfold(from_east_ref[...], rows)
    forward = []
    for k in range(own):
        values = tracer_ref[k]
        zonal = zonal_ref[k]
        merid = merid_ref[k]
        c_west = jnp.where(lane == 0, turn(from_west, -k, 1), turn(values, 1, 1))
        c_east = jnp.where(lane == width - 1, turn(from_east, width - 1 - k, 1), turn(values, -1, 1))
        u_next = jnp.where(lane == width - 1, turn(from_east, width - 1 - own - k, 1), turn(zonal, -1, 1))
        u_next_ref[k] = u_next
        flux_y = merid * (turn(values, 1, 0) + values)
        change = u_next * (values + c_east) - zonal * (c_west + values) + (turn(flux_y, -1, 0) - flux_y)
        forward.append(jnp.where(wet_levels > first + k, values - HALF_STEP * change, 0.0))

    thick = [splat(thick_ref[first + k], width) for k in range(own)]
    conduct = [None]
    for k in range(1, own):
        conduct.append(
            conductance(forward[k] - forward[k - 1], thick[k - 1], thick[k], wet_levels > first + k)
        )
    pivot = jnp.broadcast_to(thick[0], (rows, width))
    ratio, scale = [None], []
    g_forward = [thick[0] * forward[0]]
    g_adjoint = [cot_ref[0]]
    g_top = [jnp.ones((rows, width), jnp.float32)]
    for k in range(1, own):
        inverse = 1.0 / (pivot + conduct[k])
        scale.append(inverse)
        ratio.append(conduct[k] * inverse)
        pivot = thick[k] + pivot * ratio[k]
        g_forward.append(thick[k] * forward[k] + ratio[k] * g_forward[k - 1])
        g_adjoint.append(cot_ref[k] + ratio[k] * g_adjoint[k - 1])
        g_top.append(ratio[k] * g_top[k - 1])
    scale.append(1.0 / pivot)
    last = own - 1
    y_forward = g_forward[last] * scale[last]
    y_adjoint = g_adjoint[last] * scale[last]
    y_top = g_top[last] * scale[last]
    y_bottom = scale[last]
    block_ref[1] = y_top
    block_ref[2] = y_bottom
    block_ref[4] = y_forward
    block_ref[6] = y_adjoint
    block_ref[7] = forward[0]
    block_ref[8] = forward[last]
    sums = [jnp.zeros((rows, width), jnp.float32)] * 3
    for k in range(last, -1, -1):
        if k < last:
            y_forward = g_forward[k] * scale[k] + ratio[k + 1] * y_forward
            y_adjoint = g_adjoint[k] * scale[k] + ratio[k + 1] * y_adjoint
            y_top = g_top[k] * scale[k] + ratio[k + 1] * y_top
            y_bottom = ratio[k + 1] * y_bottom
        forward_ref[k] = y_forward
        adjoint_ref[k] = y_adjoint
        top_ref[k] = y_top
        bottom_ref[k] = y_bottom
        square = thick[k] * thick[k]
        sums = [s + square * y for s, y in zip(sums, (y_adjoint, y_top, y_bottom))]
    block_ref[0] = y_top
    block_ref[3] = y_forward
    block_ref[5] = y_adjoint
    block_ref[9] = sums[0]
    block_ref[10] = sums[1]
    block_ref[11] = sums[2]

    def add_level(k, total):
        return total + jnp.where(wet_levels > k, thick_ref[k], 0.0)

    depth = lax.fori_loop(0, level_count, add_level, jnp.zeros((rows, width), jnp.float32), unroll=8)
    damping_ref[...] = 0.3 + depth / level_count


def merge_kernel(size, final, own, thick_ref, wet_ref, mine_ref, other_ref, block_ref, flux_ref):
    place = lax.axis_index("lev")
    width = wet_ref.shape[1]
    upper = lax.rem(place // size, 2) == 0
    above = [jnp.where(upper, mine_ref[i], other_ref[i]) for i in range(N_BLOCK)]
    below = [jnp.where(upper, other_ref[i], mine_ref[i]) for i in range(N_BLOCK)]
    start = (place // (2 * size) * 2 + 1) * size * own
    rate = conductance(
        below[7] - above[8],
        splat(thick_ref[start - 1], width),
        splat(thick_ref[start], width),
        wet_ref[...] > start,
    )
    rate = rate / (1.0 + rate * (below[0] + above[2]))
    by_forward = rate * (below[3] - above[4])
    by_adjoint = rate * (below[5] - above[6])
    by_top = -rate * above[1]
    by_bottom = rate * below[1]
    flux_ref[0] = by_forward
    flux_ref[1] = by_adjoint
    flux_ref[2] = by_top
    flux_ref[3] = by_bottom
    spread = above[11] - below[10]
    merged = [
        above[0] + above[1] * by_top,
        -below[1] * by_top,
        below[2] - below[1] * by_bottom,
        above[3] + above[1] * by_forward,
        below[4] - below[1] * by_forward,
        above[5] + above[1] * by_adjoint,
        below[6] - below[1] * by_adjoint,
        above[7],
        below[8],
        above[9] + below[9] + by_adjoint * spread,
        above[10] + by_top * spread,
        below[11] + by_bottom * spread,
    ]
    if final:
        upper_next = lax.rem(place // (2 * size), 2) == 0
        merged = last_fields(upper_next, merged)
    for i, field in enumerate(merged):
        block_ref[i] = field


def last_fields(upper, block):
    return [
        jnp.where(upper, block[2], block[0]),
        jnp.where(upper, block[4], block[3]),
        jnp.where(upper, block[6], block[5]),
        jnp.where(upper, block[8], block[7]),
        block[9],
        jnp.where(upper, block[11], block[10]),
    ]


def pick_kernel(size, block_ref, out_ref):
    upper = lax.rem(lax.axis_index("lev") // size, 2) == 0
    block = [block_ref[i] for i in range(N_BLOCK)]
    for i, field in enumerate(last_fields(upper, block)):
        out_ref[i] = field


def final_kernel(
    sizes, own, thick_ref, wet_ref, mine_ref, other_ref, adjoint_ref, top_ref, bottom_ref, damping_ref, *rest
):
    flux_refs, message_ref, ends_ref, pulled_ref = rest[:-3], rest[-3], rest[-2], rest[-1]
    rows, width = wet_ref.shape
    place = lax.axis_index("lev")
    size = sizes[-1]
    upper = lax.rem(place // size, 2) == 0
    start = (place // (2 * size) * 2 + 1) * size * own
    wet_levels = wet_ref[...]
    rate = conductance(
        mine_ref[3] - other_ref[3],
        splat(thick_ref[start - 1], width),
        splat(thick_ref[start], width),
        wet_levels > start,
    )
    rate = rate / (1.0 + rate * (mine_ref[0] + other_ref[0]))
    in_forward = rate * (other_ref[1] - mine_ref[1])
    in_adjoint = rate * (other_ref[2] - mine_ref[2])
    source = mine_ref[4] + other_ref[4] + in_adjoint * (mine_ref[5] - other_ref[5])
    ends = []
    for into, index in ((in_forward, 0), (in_adjoint, 1)):
        top = jnp.where(upper, 0.0, into)
        bottom = jnp.where(upper, into, 0.0)
        for step in range(len(sizes) - 2, -1, -1):
            flux_ref = flux_refs[step]
            flux = flux_ref[index] + top * flux_ref[2] + bottom * flux_ref[3]
            above = lax.rem(place // sizes[step], 2) == 0
            top, bottom = jnp.where(above, top, -flux), jnp.where(above, flux, bottom)
        ends += [top, bottom]
    for i in range(4):
        ends_ref[i] = ends[i]
    lane = lanes(rows, width)
    first = place * own
    edges = jnp.zeros((rows, width), jnp.float32)
    for k in range(own):
        mixed = adjoint_ref[k] + top_ref[k] * ends[2] + bottom_ref[k] * ends[3]
        pulled = jnp.where(wet_levels > first + k, thick_ref[first + k] * mixed, 0.0)
        pulled_ref[k] = pulled
        edges = jnp.where(lane == k, turn(pulled, k, 1), edges)
        edges = jnp.where(lane == own + k, turn(pulled, own + k + 1, 1), edges)
    message_ref[:rows] = source
    message_ref[rows : rows + 8] = fold(edges)
    message_ref[rows + 8 :] = damping_ref[...]


def forward_kernel(forward_ref, top_ref, bottom_ref, ends_ref, out_ref):
    top = ends_ref[0]
    bottom = ends_ref[1]
    for k in range(forward_ref.shape[0]):
        out_ref[k] = forward_ref[k] + top_ref[k] * top + bottom_ref[k] * bottom


def total(field):
    while field.ndim > 2:
        field = jnp.sum(field, axis=0)
    return jnp.sum(jnp.sum(field, axis=0, keepdims=True), axis=1, keepdims=True)


def surface_kernel(
    pulled_ref, zonal_ref, merid_ref, u_next_ref, messages_ref, tracer_adjoint_ref, surface_ref,
    source_scr, damping_scr,
):
    own, rows, width = pulled_ref.shape
    count = messages_ref.shape[0]
    place = lax.axis_index("sub")
    lane = lanes(rows, width)
    for i in range(count):
        owner = jnp.bitwise_xor(place, i)
        source_scr[owner] = messages_ref[i, :rows]
        damping_scr[owner] = messages_ref[i, rows + 8 :]
    west_of = jnp.bitwise_xor(place, lax.rem(place + count - 1, count))
    east_of = jnp.bitwise_xor(place, lax.rem(place + 1, count))
    west_edges = unfold(messages_ref[west_of, rows : rows + 8], rows)
    east_edges = unfold(messages_ref[east_of, rows : rows + 8], rows)
    for k in range(own):
        pulled = pulled_ref[k]
        merid = merid_ref[k]
        b_west = jnp.where(lane == 0, turn(west_edges, -own - k, 1), turn(pulled, 1, 1))
        b_east = jnp.where(lane == width - 1, turn(east_edges, width - 1 - k, 1), turn(pulled, -1, 1))
        across = zonal_ref[k] * (pulled - b_west) + u_next_ref[k] * (b_east - pulled)
        step = merid * (pulled - turn(pulled, 1, 0))
        across = across + step + turn(step, -1, 0)
        tracer_adjoint_ref[k] = pulled + HALF_STEP * across

    first_lane = lax.broadcasted_iota(jnp.int32, (count, rows, width), 2) == 0
    last_lane = lax.broadcasted_iota(jnp.int32, (count, rows, width), 2) == width - 1
    damping = 4.0 + damping_scr[...]

    def beside(field, shift):
        return jnp.concatenate([field[-shift:], field[:-shift]]) if count > 1 else field

    def image_of(field):
        west = turn(field, 1, 2)
        west = jnp.where(first_lane, beside(west, 1), west)
        east = turn(field, -1, 2)
        east = jnp.where(last_lane, beside(east, -1), east)
        return damping * field - (west + east + turn(field, 1, 1) + turn(field, -1, 1))

    residual = source_scr[...]
    image = image_of(residual)
    norm = total(residual * residual)
    step_size = norm / total(residual * image)
    direction, along = residual, image
    surface = jnp.zeros_like(residual)
    for sweep in range(ITERS):
        surface = surface + step_size * direction
        if sweep + 1 < ITERS:
            residual = residual - step_size * along
            image = image_of(residual)
            norm_next = total(residual * residual)
            product = total(residual * image)
            growth = norm_next / norm
            step_size = norm_next / (product - growth * norm_next / step_size)
            direction = residual + growth * direction
            along = image + growth * along
            norm = norm_next
    source_scr[...] = surface
    surface_ref[...] = source_scr[place]


def on_device(tracer, zonal_flow, meridional_flow, cotangent, thickness, wet_levels):
    own, rows, width = tracer.shape
    lev_count = lax.axis_size("lev")
    sub_count = lax.axis_size("sub")
    edge = in_vmem(rows, width)
    thickness = pltpu.with_memory_space_constraint(thickness, pltpu.SMEM)
    levels = in_vmem(own, rows, width)

    tracer, zonal_flow, wet_levels, east, west = pl.pallas_call(
        pack_kernel,
        out_shape=(levels, levels, pltpu.VMEM((rows, width), jnp.int32), in_vmem(8, width), in_vmem(8, width)),
        in_specs=[pl.BlockSpec(memory_space=pl.ANY)] * 3,
        out_specs=(VMEM_IN,) * 5,
        scratch_shapes=[pltpu.SemaphoreType.DMA((3,))],
        name="pack",
    )(tracer, zonal_flow, wet_levels)
    ring = [(i, (i + 1) % sub_count) for i in range(sub_count)]
    from_west = lax.ppermute(east, "sub", ring)
    from_east = lax.ppermute(west, "sub", [(b, a) for a, b in ring])

    block, forward, adjoint, top, bottom, u_next, damping = pl.pallas_call(
        local_kernel,
        out_shape=(in_vmem(N_BLOCK, rows, width), levels, levels, levels, levels, levels, edge),
        in_specs=[SMEM_IN] + [VMEM_IN] * 7,
        out_specs=(VMEM_IN,) * 7,
        name="local",
    )(thickness, *near(wet_levels, tracer, zonal_flow, meridional_flow, cotangent, from_west, from_east))

    sizes = [1]
    while sizes[-1] * 2 < lev_count:
        sizes.append(sizes[-1] * 2)
    fluxes = []
    if len(sizes) == 1:
        block = pl.pallas_call(
            functools.partial(pick_kernel, 1), out_shape=in_vmem(N_LAST, rows, width),
            in_specs=[VMEM_IN], out_specs=VMEM_IN, name="pick",
        )(*near(block))
    for size in sizes:
        other = lax.ppermute(block, "lev", [(i, i ^ size) for i in range(lev_count)])
        if size == sizes[-1]:
            break
        final = size * 2 == sizes[-1]
        block, flux = pl.pallas_call(
            functools.partial(merge_kernel, size, final, own),
            out_shape=(in_vmem(N_LAST if final else N_BLOCK, rows, width), in_vmem(4, rows, width)),
            in_specs=[SMEM_IN] + [VMEM_IN] * 3,
            out_specs=(VMEM_IN,) * 2,
            name="merge",
        )(thickness, *near(wet_levels, block, other))
        fluxes.append(flux)

    message, ends, pulled = pl.pallas_call(
        functools.partial(final_kernel, sizes, own),
        out_shape=(in_vmem(2 * rows + 8, width), in_vmem(4, rows, width), levels),
        in_specs=[SMEM_IN] + [VMEM_IN] * (7 + len(fluxes)),
        out_specs=(VMEM_IN,) * 3,
        name="final",
    )(thickness, *near(wet_levels, block, other, adjoint, top, bottom, damping, *fluxes))

    messages = message[None]
    size = 1
    while size < sub_count:
        got = lax.ppermute(messages, "sub", [(i, i ^ size) for i in range(sub_count)])
        messages = jnp.concatenate([messages, got])
        size *= 2

    next_tracer = pl.pallas_call(
        forward_kernel,
        out_shape=jax.ShapeDtypeStruct(tracer.shape, jnp.float32),
        in_specs=[VMEM_IN] * 4,
        out_specs=VMEM_IN,
        name="forward",
    )(*near(forward, top, bottom, ends))

    tracer_adjoint, surface = pl.pallas_call(
        surface_kernel,
        out_shape=(
            jax.ShapeDtypeStruct(tracer.shape, jnp.float32),
            jax.ShapeDtypeStruct((rows, width), jnp.float32),
        ),
        in_specs=[VMEM_IN] * 5,
        out_specs=(VMEM_IN,) * 2,
        scratch_shapes=[pltpu.VMEM((sub_count, rows, width), jnp.float32)] * 2,
        name="surface",
    )(*near(pulled, zonal_flow, meridional_flow, u_next, messages))
    return (next_tracer, tracer_adjoint, surface)


def solution(mesh):
    whole = P(("members", "lev"), None, "sub")
    return jax.shard_map(
        on_device,
        mesh=mesh,
        in_specs=(whole, whole, whole, whole, P(), P(None, "sub")),
        out_specs=(whole, whole, P("members", "sub")),
        check_vma=False,
    )
```

```python
import functools

import jax
import jax.numpy as jnp
from jax import lax
from jax.experimental import pallas as pl
from jax.experimental.pallas import tpu as pltpu
from jax.sharding import PartitionSpec as P

ITERS = 3
ADVECT_STEP = 0.25
MIX_RATE = 2.0
HALF_STEP = 0.5 * ADVECT_STEP

N_BLOCK = 12
N_LAST = 6

VMEM_IN = pl.BlockSpec(memory_space=pltpu.VMEM)
SMEM_IN = pl.BlockSpec(memory_space=pltpu.SMEM)


def in_vmem(*shape):
    return pltpu.VMEM(shape, jnp.float32)


def near(*arrays):
    return [pltpu.with_memory_space_constraint(array, pltpu.VMEM) for array in arrays]


def lanes(rows, width):
    return lax.broadcasted_iota(jnp.int32, (rows, width), 1)


def turn(field, shift, axis):
    size = field.shape[axis]
    shift = shift % size
    return field if shift == 0 else pltpu.roll(field, shift, axis)


def splat(scalar, width):
    return jnp.full((1, width), scalar, jnp.float32)


def conductance(drop, upper_thick, lower_thick, wet):
    spacing = 0.5 * (upper_thick + lower_thick)
    rate = 0.2 / spacing + spacing / (spacing * spacing + drop * drop)
    return jnp.where(wet, MIX_RATE * rate, 0.0)


def parity(width):
    return lax.rem(lanes(8, width), 2)


def fold_edges(levels):
    rows, width = levels[0].shape
    groups = rows // 8
    slot = width // groups
    pair = lanes(8, width) // 2
    folded = jnp.zeros((8, width), levels[0].dtype)
    for k, field in enumerate(levels):
        for group in range(groups):
            place = slot * group + 2 * k
            turned = turn(field[8 * group : 8 * group + 8], place + 1, 1)
            folded = jnp.where(pair == place // 2, turned, folded)
    return folded


def fold_surface(field):
    rows, width = field.shape
    groups = rows // 8
    slot = width // groups
    group_of = lanes(8, width) // slot
    folded = jnp.zeros((8, width), field.dtype)
    for group in range(groups):
        part = field[8 * group : 8 * group + 8]
        ends = jnp.where(
            parity(width) == 0,
            jnp.broadcast_to(part[:, width - 1 :], part.shape),
            jnp.broadcast_to(part[:, :1], part.shape),
        )
        folded = jnp.where(group_of == group, ends, folded)
    return folded


def beside_edges(from_west, from_east):
    return jnp.where(parity(from_west.shape[1]) == 0, turn(from_east, -1, 1), turn(from_west, 1, 1))


def spread_edges(beside, rows, k):
    width = beside.shape[1]
    groups = rows // 8
    slot = width // groups
    return jnp.concatenate([turn(beside, -(slot * group + 2 * k + 1), 1) for group in range(groups)])


def pack_kernel(
    tracer_hbm, zonal_hbm, wet_hbm, tracer_ref, zonal_ref, wet_ref, east_ref, west_ref, zonal_edges_ref, sems
):
    own = tracer_ref.shape[0]
    copies = [
        pltpu.make_async_copy(source, target, sems.at[i])
        for i, (source, target) in enumerate(
            ((tracer_hbm, tracer_ref), (zonal_hbm, zonal_ref), (wet_hbm, wet_ref))
        )
    ]
    for copy in copies:
        copy.start()
    copies[0].wait()
    east = fold_edges([tracer_ref[k] for k in range(own)])
    east_ref[:8] = east
    east_ref[8:] = east
    west_ref[:8] = east
    copies[1].wait()
    zonal_edges = fold_edges([zonal_ref[k] for k in range(own)])
    west_ref[8:] = zonal_edges
    zonal_edges_ref[...] = zonal_edges
    copies[2].wait()


def prepare_kernel(own, thick_ref, wet_ref, rows_ref, damping_ref, weight_ref):
    level_count = thick_ref.shape[0]
    rows, width = wet_ref.shape
    wet_levels = wet_ref[...]
    depth = jnp.zeros((rows, width), jnp.float32)
    for k in range(level_count):
        thick = splat(thick_ref[k], width)
        rows_ref[k : k + 1] = thick
        depth = depth + jnp.where(wet_levels > k, thick, 0.0)
    damping_ref[...] = 0.3 + depth / level_count
    wet_edges = fold_surface(wet_levels)
    offset = lax.rem(lanes(8, width), width // (rows // 8)) // 2
    first = lax.axis_index("lev") * own
    thick = jnp.zeros((8, width), jnp.float32)
    for k in range(own):
        thick = jnp.where(offset == k, thick_ref[first + k], thick)
    weight_ref[...] = jnp.where(wet_edges > offset + first, thick, 0.0)


def local_kernel(
    thick_ref, wet_ref, tracer_ref, zonal_ref, merid_ref, cot_ref, from_west_ref, from_east_ref,
    zonal_edges_ref, block_ref, forward_ref, adjoint_ref, top_ref, bottom_ref, u_next_ref, factor_ref, edges_ref,
):
    own, rows, width = tracer_ref.shape
    first = lax.axis_index("lev") * own
    lane = lanes(rows, width)
    wet_levels = wet_ref[...]
    beside = beside_edges(from_west_ref[:8], from_east_ref[:8])
    beside_zonal = turn(from_east_ref[8:], -1, 1)
    factor_ref[...] = HALF_STEP * jnp.where(parity(width) == 0, beside_zonal, -zonal_edges_ref[...])
    forward = []
    for k in range(own):
        values = tracer_ref[k]
        zonal = zonal_ref[k]
        merid = merid_ref[k]
        edge = spread_edges(beside, rows, k)
        c_west = jnp.where(lane == 0, edge, turn(values, 1, 1))
        c_east = jnp.where(lane == width - 1, edge, turn(values, -1, 1))
        u_next = jnp.where(lane == width - 1, spread_edges(beside_zonal, rows, k), turn(zonal, -1, 1))
        u_next_ref[k] = u_next
        flux_y = merid * (turn(values, 1, 0) + values)
        change = u_next * (values + c_east) - zonal * (c_west + values) + (turn(flux_y, -1, 0) - flux_y)
        forward.append(jnp.where(wet_levels > first + k, values - HALF_STEP * change, 0.0))

    thick = [thick_ref[pl.ds(first + k, 1)] for k in range(own)]
    conduct = [None]
    for k in range(1, own):
        conduct.append(
            conductance(forward[k] - forward[k - 1], thick[k - 1], thick[k], wet_levels > first + k)
        )
    pivot = jnp.broadcast_to(thick[0], (rows, width))
    ratio, scale = [None], []
    g_forward = [thick[0] * forward[0]]
    g_adjoint = [cot_ref[0]]
    g_top = [jnp.ones((rows, width), jnp.float32)]
    for k in range(1, own):
        inverse = 1.0 / (pivot + conduct[k])
        scale.append(inverse)
        ratio.append(conduct[k] * inverse)
        pivot = thick[k] + pivot * ratio[k]
        g_forward.append(thick[k] * forward[k] + ratio[k] * g_forward[k - 1])
        g_adjoint.append(cot_ref[k] + ratio[k] * g_adjoint[k - 1])
        g_top.append(ratio[k] * g_top[k - 1])
    scale.append(1.0 / pivot)

    def put(index, field):
        block_ref[rows * index : rows * (index + 1)] = field

    last = own - 1
    y_forward = g_forward[last] * scale[last]
    y_adjoint = g_adjoint[last] * scale[last]
    y_top = g_top[last] * scale[last]
    y_bottom = scale[last]
    put(1, y_top)
    put(2, y_bottom)
    put(4, y_forward)
    put(6, y_adjoint)
    put(7, forward[0])
    put(8, forward[last])
    sums = [jnp.zeros((rows, width), jnp.float32)] * 3
    for k in range(last, -1, -1):
        if k < last:
            y_forward = g_forward[k] * scale[k] + ratio[k + 1] * y_forward
            y_adjoint = g_adjoint[k] * scale[k] + ratio[k + 1] * y_adjoint
            y_top = g_top[k] * scale[k] + ratio[k + 1] * y_top
            y_bottom = ratio[k + 1] * y_bottom
        forward_ref[k] = y_forward
        adjoint_ref[k] = y_adjoint
        top_ref[k] = y_top
        bottom_ref[k] = y_bottom
        square = thick[k] * thick[k]
        sums = [s + square * y for s, y in zip(sums, (y_adjoint, y_top, y_bottom))]
    put(0, y_top)
    put(3, y_forward)
    put(5, y_adjoint)
    for i in range(3):
        put(9 + i, sums[i])
    for i, ref in enumerate((adjoint_ref, top_ref, bottom_ref)):
        edges_ref[8 * i : 8 * i + 8] = fold_edges([ref[k] for k in range(own)])


def merge_kernel(size, final, own, thick_ref, wet_ref, mine_ref, other_ref, block_ref, flux_ref):
    place = lax.axis_index("lev")
    rows, width = wet_ref.shape
    upper = lax.rem(place // size, 2) == 0
    mine = [mine_ref[rows * i : rows * (i + 1)] for i in range(N_BLOCK)]
    other = [other_ref[rows * i : rows * (i + 1)] for i in range(N_BLOCK)]
    above = [jnp.where(upper, a, b) for a, b in zip(mine, other)]
    below = [jnp.where(upper, b, a) for a, b in zip(mine, other)]
    start = (place // (2 * size) * 2 + 1) * size * own
    rate = conductance(
        below[7] - above[8],
        thick_ref[pl.ds(start - 1, 1)],
        thick_ref[pl.ds(start, 1)],
        wet_ref[...] > start,
    )
    rate = rate / (1.0 + rate * (below[0] + above[2]))
    by_forward = rate * (below[3] - above[4])
    by_adjoint = rate * (below[5] - above[6])
    by_top = -rate * above[1]
    by_bottom = rate * below[1]
    flux_ref[0] = by_forward
    flux_ref[1] = by_adjoint
    flux_ref[2] = by_top
    flux_ref[3] = by_bottom
    spread = above[11] - below[10]
    merged = [
        above[0] + above[1] * by_top,
        -below[1] * by_top,
        below[2] - below[1] * by_bottom,
        above[3] + above[1] * by_forward,
        below[4] - below[1] * by_forward,
        above[5] + above[1] * by_adjoint,
        below[6] - below[1] * by_adjoint,
        above[7],
        below[8],
        above[9] + below[9] + by_adjoint * spread,
        above[10] + by_top * spread,
        below[11] + by_bottom * spread,
    ]
    if final:
        upper_next = lax.rem(place // (2 * size), 2) == 0
        merged = last_fields(upper_next, merged)
    for i, field in enumerate(merged):
        block_ref[rows * i : rows * (i + 1)] = field


def last_fields(upper, block):
    return [
        jnp.where(upper, block[2], block[0]),
        jnp.where(upper, block[4], block[3]),
        jnp.where(upper, block[6], block[5]),
        jnp.where(upper, block[8], block[7]),
        block[9],
        jnp.where(upper, block[11], block[10]),
    ]


def final_kernel(
    sizes, own, thick_ref, wet_ref, weight_ref, mine_ref, other_ref, edges_ref, damping_ref, *rest
):
    flux_refs, message_ref, ends_ref = rest[:-2], rest[-2], rest[-1]
    rows, width = wet_ref.shape
    place = lax.axis_index("lev")
    size = sizes[-1]
    upper = lax.rem(place // size, 2) == 0
    start = (place // (2 * size) * 2 + 1) * size * own
    mine = [mine_ref[rows * i : rows * (i + 1)] for i in range(N_LAST)]
    other = [other_ref[rows * i : rows * (i + 1)] for i in range(N_LAST)]
    rate = conductance(
        mine[3] - other[3],
        thick_ref[pl.ds(start - 1, 1)],
        thick_ref[pl.ds(start, 1)],
        wet_ref[...] > start,
    )
    rate = rate / (1.0 + rate * (mine[0] + other[0]))
    in_forward = rate * (other[1] - mine[1])
    in_adjoint = rate * (other[2] - mine[2])
    message_ref[:rows] = mine[4] + other[4] + in_adjoint * (mine[5] - other[5])
    message_ref[rows + 8 :] = damping_ref[...]
    for into, index in ((in_forward, 0), (in_adjoint, 1)):
        top = jnp.where(upper, 0.0, into)
        bottom = jnp.where(upper, into, 0.0)
        for step in range(len(sizes) - 2, -1, -1):
            flux_ref = flux_refs[step]
            flux = flux_ref[index] + top * flux_ref[2] + bottom * flux_ref[3]
            above = lax.rem(place // sizes[step], 2) == 0
            top, bottom = jnp.where(above, top, -flux), jnp.where(above, flux, bottom)
        ends_ref[2 * index] = top
        ends_ref[2 * index + 1] = bottom

    mixed = edges_ref[:8] + edges_ref[8:16] * fold_surface(top) + edges_ref[16:] * fold_surface(bottom)
    message_ref[rows : rows + 8] = weight_ref[...] * mixed


def rest_kernel(
    thick_ref, wet_ref, ends_ref, forward_ref, adjoint_ref, top_ref, bottom_ref, zonal_ref, merid_ref, u_next_ref,
    next_tracer_ref, inner_ref,
):
    own, rows, width = forward_ref.shape
    first = lax.axis_index("lev") * own
    lane = lanes(rows, width)
    wet_levels = wet_ref[...]
    ends = [ends_ref[i] for i in range(4)]
    for k in range(own):
        next_tracer_ref[k] = forward_ref[k] + top_ref[k] * ends[0] + bottom_ref[k] * ends[1]
        mixed = adjoint_ref[k] + top_ref[k] * ends[2] + bottom_ref[k] * ends[3]
        pulled = jnp.where(wet_levels > first + k, thick_ref[pl.ds(first + k, 1)] * mixed, 0.0)
        b_west = jnp.where(lane == 0, 0.0, turn(pulled, 1, 1))
        b_east = jnp.where(lane == width - 1, 0.0, turn(pulled, -1, 1))
        across = zonal_ref[k] * (pulled - b_west) + u_next_ref[k] * (b_east - pulled)
        step = merid_ref[k] * (pulled - turn(pulled, 1, 0))
        inner_ref[k] = pulled + HALF_STEP * (across + step + turn(step, -1, 0))


def total(field):
    while field.ndim > 2:
        field = jnp.sum(field, axis=0)
    return jnp.sum(jnp.sum(field, axis=0, keepdims=True), axis=1, keepdims=True)


def surface_kernel(
    gathered_ref, inner_ref, factor_ref, tracer_adjoint_ref, surface_ref,
    source_scr, damping_scr, edges_scr,
):
    own, rows, width = inner_ref.shape
    count = gathered_ref.shape[0]
    place = lax.axis_index("sub")
    for i in range(count):
        owner = jnp.bitwise_xor(place, i)
        source_scr[owner] = gathered_ref[i, :rows]
        damping_scr[owner] = gathered_ref[i, rows + 8 :]
        edges_scr[owner] = gathered_ref[i, rows : rows + 8]
    west_edges = edges_scr[lax.rem(place + count - 1, count)]
    east_edges = edges_scr[lax.rem(place + 1, count)]
    beside = factor_ref[...] * beside_edges(west_edges, east_edges)
    lane = lanes(rows, width)
    at_edge = jnp.logical_or(lane == 0, lane == width - 1)
    for k in range(own):
        tracer_adjoint_ref[k] = inner_ref[k] + jnp.where(at_edge, spread_edges(beside, rows, k), 0.0)

    first_lane = lax.broadcasted_iota(jnp.int32, (count, rows, width), 2) == 0
    last_lane = lax.broadcasted_iota(jnp.int32, (count, rows, width), 2) == width - 1
    damping = 4.0 + damping_scr[...]

    def passed(field, shift):
        return jnp.concatenate([field[-shift:], field[:-shift]]) if count > 1 else field

    def image_of(field):
        west = turn(field, 1, 2)
        west = jnp.where(first_lane, passed(west, 1), west)
        east = turn(field, -1, 2)
        east = jnp.where(last_lane, passed(east, -1), east)
        return damping * field - (west + east + turn(field, 1, 1) + turn(field, -1, 1))

    residual = source_scr[...]
    image = image_of(residual)
    norm = total(residual * residual)
    step_size = norm / total(residual * image)
    direction, along = residual, image
    surface = jnp.zeros_like(residual)
    for sweep in range(ITERS):
        surface = surface + step_size * direction
        if sweep + 1 < ITERS:
            residual = residual - step_size * along
            image = image_of(residual)
            norm_next = total(residual * residual)
            product = total(residual * image)
            growth = norm_next / norm
            step_size = norm_next / (product - growth * norm_next / step_size)
            direction = residual + growth * direction
            along = image + growth * along
            norm = norm_next
    source_scr[...] = surface
    surface_ref[...] = source_scr[place]


def on_device(tracer, zonal_flow, meridional_flow, cotangent, thickness, wet_levels):
    own, rows, width = tracer.shape
    lev_count = lax.axis_size("lev")
    sub_count = lax.axis_size("sub")
    edge = in_vmem(rows, width)
    levels = in_vmem(own, rows, width)
    marks = pltpu.VMEM((rows, width), jnp.int32)
    thickness = pltpu.with_memory_space_constraint(thickness, pltpu.SMEM)

    tracer, zonal_flow, wet_levels, east, west, zonal_edges = pl.pallas_call(
        pack_kernel,
        out_shape=(levels, levels, marks, in_vmem(16, width), in_vmem(16, width), in_vmem(8, width)),
        in_specs=[pl.BlockSpec(memory_space=pl.ANY)] * 3,
        out_specs=(VMEM_IN,) * 6,
        scratch_shapes=[pltpu.SemaphoreType.DMA((3,))],
        name="pack",
    )(tracer, zonal_flow, wet_levels)
    ring = [(i, (i + 1) % sub_count) for i in range(sub_count)]
    from_west = lax.ppermute(east, "sub", ring)
    from_east = lax.ppermute(west, "sub", [(b, a) for a, b in ring])
    thickness, damping, weights = pl.pallas_call(
        functools.partial(prepare_kernel, own),
        out_shape=(in_vmem(thickness.shape[0], width), edge, in_vmem(8, width)),
        in_specs=[SMEM_IN, VMEM_IN],
        out_specs=(VMEM_IN,) * 3,
        name="prepare",
    )(thickness, *near(wet_levels))

    block, forward, adjoint, top, bottom, u_next, factor, edges = pl.pallas_call(
        local_kernel,
        out_shape=(in_vmem(N_BLOCK * rows, width), levels, levels, levels, levels, levels, in_vmem(8, width), in_vmem(24, width)),
        in_specs=[VMEM_IN] * 9,
        out_specs=(VMEM_IN,) * 8,
        name="local",
    )(*near(thickness, wet_levels, tracer, zonal_flow, meridional_flow, cotangent, from_west, from_east, zonal_edges))

    sizes = [1]
    while sizes[-1] * 2 < lev_count:
        sizes.append(sizes[-1] * 2)
    fluxes = []
    for size in sizes:
        other = lax.ppermute(block, "lev", [(i, i ^ size) for i in range(lev_count)])
        if size == sizes[-1]:
            break
        final = size * 2 == sizes[-1]
        block, flux = pl.pallas_call(
            functools.partial(merge_kernel, size, final, own),
            out_shape=(in_vmem((N_LAST if final else N_BLOCK) * rows, width), in_vmem(4, rows, width)),
            in_specs=[VMEM_IN] * 4,
            out_specs=(VMEM_IN,) * 2,
            name="merge",
        )(*near(thickness, wet_levels, block, other))
        fluxes.append(flux)

    message, ends = pl.pallas_call(
        functools.partial(final_kernel, sizes, own),
        out_shape=(in_vmem(2 * rows + 8, width), in_vmem(4, rows, width)),
        in_specs=[VMEM_IN] * (7 + len(fluxes)),
        out_specs=(VMEM_IN,) * 2,
        name="final",
    )(*near(thickness, wet_levels, weights, block, other, edges, damping, *fluxes))

    gathered = message[None]
    size = 1
    while size < sub_count:
        got = lax.ppermute(gathered, "sub", [(i, i ^ size) for i in range(sub_count)])
        gathered = jnp.concatenate([gathered, got])
        size *= 2

    next_tracer, inner = pl.pallas_call(
        rest_kernel,
        out_shape=(jax.ShapeDtypeStruct(tracer.shape, jnp.float32), levels),
        in_specs=[VMEM_IN] * 10,
        out_specs=(VMEM_IN,) * 2,
        name="rest",
    )(*near(thickness, wet_levels, ends, forward, adjoint, top, bottom, zonal_flow, meridional_flow, u_next))

    tracer_adjoint, surface = pl.pallas_call(
        surface_kernel,
        out_shape=(
            jax.ShapeDtypeStruct(tracer.shape, jnp.float32),
            jax.ShapeDtypeStruct((rows, width), jnp.float32),
        ),
        in_specs=[VMEM_IN] * 3,
        out_specs=(VMEM_IN,) * 2,
        scratch_shapes=[pltpu.VMEM((sub_count, rows, width), jnp.float32)] * 2
        + [pltpu.VMEM((sub_count, 8, width), jnp.float32)],
        name="surface",
    )(*near(gathered, inner, factor))
    return (next_tracer, tracer_adjoint, surface)


def solution(mesh):
    whole = P(("members", "lev"), None, "sub")
    return jax.shard_map(
        on_device,
        mesh=mesh,
        in_specs=(whole, whole, whole, whole, P(), P(None, "sub")),
        out_specs=(whole, whole, P("members", "sub")),
        check_vma=False,
    )
```

```python
import functools

import jax
import jax.numpy as jnp
from jax import lax
from jax.experimental import pallas as pl
from jax.experimental.pallas import tpu as pltpu
from jax.sharding import PartitionSpec as P

ITERS = 3
ADVECT_STEP = 0.25
MIX_RATE = 2.0
HALF_STEP = 0.5 * ADVECT_STEP

N_BLOCK = 12
N_LAST = 6

VMEM_IN = pl.BlockSpec(memory_space=pltpu.VMEM)
SMEM_IN = pl.BlockSpec(memory_space=pltpu.SMEM)


def in_vmem(*shape):
    return pltpu.VMEM(shape, jnp.float32)


def near(*arrays):
    return [pltpu.with_memory_space_constraint(array, pltpu.VMEM) for array in arrays]


def lanes(rows, width):
    return lax.broadcasted_iota(jnp.int32, (rows, width), 1)


def turn(field, shift, axis):
    size = field.shape[axis]
    shift = shift % size
    return field if shift == 0 else pltpu.roll(field, shift, axis)


def splat(scalar, width):
    return jnp.full((1, width), scalar, jnp.float32)


def conductance(drop, upper_thick, lower_thick, wet):
    spacing = 0.5 * (upper_thick + lower_thick)
    rate = 0.2 / spacing + spacing / (spacing * spacing + drop * drop)
    return jnp.where(wet, MIX_RATE * rate, 0.0)


def parity(width):
    return lax.rem(lanes(8, width), 2)


def fold_edges(levels):
    rows, width = levels[0].shape
    groups = rows // 8
    slot = width // groups
    pair = lanes(8, width) // 2
    folded = jnp.zeros((8, width), levels[0].dtype)
    for k, field in enumerate(levels):
        for group in range(groups):
            place = slot * group + 2 * k
            turned = turn(field[8 * group : 8 * group + 8], place + 1, 1)
            folded = jnp.where(pair == place // 2, turned, folded)
    return folded


def fold_surface(field):
    rows, width = field.shape
    groups = rows // 8
    slot = width // groups
    group_of = lanes(8, width) // slot
    folded = jnp.zeros((8, width), field.dtype)
    for group in range(groups):
        part = field[8 * group : 8 * group + 8]
        ends = jnp.where(
            parity(width) == 0,
            jnp.broadcast_to(part[:, width - 1 :], part.shape),
            jnp.broadcast_to(part[:, :1], part.shape),
        )
        folded = jnp.where(group_of == group, ends, folded)
    return folded


def beside_edges(from_west, from_east):
    return jnp.where(parity(from_west.shape[1]) == 0, turn(from_east, -1, 1), turn(from_west, 1, 1))


def spread_edges(beside, rows, k):
    width = beside.shape[1]
    groups = rows // 8
    slot = width // groups
    return jnp.concatenate([turn(beside, -(slot * group + 2 * k + 1), 1) for group in range(groups)])


def pack_kernel(
    tracer_hbm, zonal_hbm, wet_hbm, tracer_ref, zonal_ref, wet_ref, east_ref, west_ref, edges_ref, sems
):
    own = tracer_ref.shape[0]
    copies = [
        pltpu.make_async_copy(source, target, sems.at[i])
        for i, (source, target) in enumerate(
            ((tracer_hbm, tracer_ref), (zonal_hbm, zonal_ref), (wet_hbm, wet_ref))
        )
    ]
    for copy in copies:
        copy.start()
    copies[0].wait()
    east = fold_edges([tracer_ref[k] for k in range(own)])
    copies[1].wait()
    zonal = fold_edges([zonal_ref[k] for k in range(own)])
    for ref in (east_ref, west_ref, edges_ref):
        ref[:8] = east
        ref[8:] = zonal
    copies[2].wait()


def prepare_kernel(
    own, thick_ref, wet_ref, tracer_ref, zonal_ref, merid_ref, rows_ref, damping_ref, weight_ref, inside_ref
):
    level_count = thick_ref.shape[0]
    rows, width = wet_ref.shape
    wet_levels = wet_ref[...]
    depth = jnp.zeros((rows, width), jnp.float32)
    for k in range(level_count):
        thick = splat(thick_ref[k], width)
        rows_ref[k : k + 1] = thick
        depth = depth + jnp.where(wet_levels > k, thick, 0.0)
    damping_ref[...] = 0.3 + depth / level_count
    wet_edges = fold_surface(wet_levels)
    offset = lax.rem(lanes(8, width), width // (rows // 8)) // 2
    first = lax.axis_index("lev") * own
    thick = jnp.zeros((8, width), jnp.float32)
    for k in range(own):
        thick = jnp.where(offset == k, thick_ref[first + k], thick)
    weight_ref[...] = jnp.where(wet_edges > offset + first, thick, 0.0)
    lane = lanes(rows, width)
    for k in range(own):
        values = tracer_ref[k]
        zonal = zonal_ref[k]
        c_west = jnp.where(lane == 0, 0.0, turn(values, 1, 1))
        u_next = jnp.where(lane == width - 1, 0.0, turn(zonal, -1, 1))
        flux_y = merid_ref[k] * (turn(values, 1, 0) + values)
        change = u_next * (values + turn(values, -1, 1)) - zonal * (c_west + values) + (turn(flux_y, -1, 0) - flux_y)
        inside_ref[k] = jnp.where(wet_levels > first + k, values - HALF_STEP * change, 0.0)


def local_kernel(
    thick_ref, wet_ref, weight_ref, inside_ref, cot_ref, edges_ref, from_west_ref, from_east_ref,
    block_ref, forward_ref, adjoint_ref, top_ref, bottom_ref, factor_ref,
):
    own, rows, width = cot_ref.shape
    first = lax.axis_index("lev") * own
    lane = lanes(rows, width)
    at_edge = jnp.logical_or(lane == 0, lane == width - 1)
    even = parity(width) == 0
    wet_levels = wet_ref[...]
    factor = HALF_STEP * jnp.where(even, turn(from_east_ref[8:], -1, 1), -edges_ref[8:])
    factor_ref[...] = factor
    beside = beside_edges(from_west_ref[:8], from_east_ref[:8])
    beside = -factor * jnp.where(even, edges_ref[:8] + beside, beside)
    beside = jnp.where(weight_ref[...] > 0.0, beside, 0.0)
    forward = []
    for k in range(own):
        forward.append(inside_ref[k] + jnp.where(at_edge, spread_edges(beside, rows, k), 0.0))

    thick = [thick_ref[pl.ds(first + k, 1)] for k in range(own)]
    conduct = [None]
    for k in range(1, own):
        conduct.append(
            conductance(forward[k] - forward[k - 1], thick[k - 1], thick[k], wet_levels > first + k)
        )
    pivot = jnp.broadcast_to(thick[0], (rows, width))
    ratio, scale = [None], []
    g_forward = [thick[0] * forward[0]]
    g_adjoint = [cot_ref[0]]
    g_top = [jnp.ones((rows, width), jnp.float32)]
    for k in range(1, own):
        inverse = 1.0 / (pivot + conduct[k])
        scale.append(inverse)
        ratio.append(conduct[k] * inverse)
        pivot = thick[k] + pivot * ratio[k]
        g_forward.append(thick[k] * forward[k] + ratio[k] * g_forward[k - 1])
        g_adjoint.append(cot_ref[k] + ratio[k] * g_adjoint[k - 1])
        g_top.append(ratio[k] * g_top[k - 1])
    scale.append(1.0 / pivot)

    def put(index, field):
        block_ref[rows * index : rows * (index + 1)] = field

    last = own - 1
    y_forward = g_forward[last] * scale[last]
    y_adjoint = g_adjoint[last] * scale[last]
    y_top = g_top[last] * scale[last]
    y_bottom = scale[last]
    put(1, y_top)
    put(2, y_bottom)
    put(4, y_forward)
    put(6, y_adjoint)
    put(7, forward[0])
    put(8, forward[last])
    sums = [jnp.zeros((rows, width), jnp.float32)] * 3
    for k in range(last, -1, -1):
        if k < last:
            y_forward = g_forward[k] * scale[k] + ratio[k + 1] * y_forward
            y_adjoint = g_adjoint[k] * scale[k] + ratio[k + 1] * y_adjoint
            y_top = g_top[k] * scale[k] + ratio[k + 1] * y_top
            y_bottom = ratio[k + 1] * y_bottom
        forward_ref[k] = y_forward
        adjoint_ref[k] = y_adjoint
        top_ref[k] = y_top
        bottom_ref[k] = y_bottom
        square = thick[k] * thick[k]
        sums = [s + square * y for s, y in zip(sums, (y_adjoint, y_top, y_bottom))]
    put(0, y_top)
    put(3, y_forward)
    put(5, y_adjoint)
    for i in range(3):
        put(9 + i, sums[i])


def edges_kernel(adjoint_ref, top_ref, bottom_ref, edges_ref):
    for i, ref in enumerate((adjoint_ref, top_ref, bottom_ref)):
        edges_ref[8 * i : 8 * i + 8] = fold_edges([ref[k] for k in range(ref.shape[0])])


def merge_kernel(size, final, own, thick_ref, wet_ref, mine_ref, other_ref, block_ref, flux_ref):
    place = lax.axis_index("lev")
    rows, width = wet_ref.shape
    upper = lax.rem(place // size, 2) == 0
    mine = [mine_ref[rows * i : rows * (i + 1)] for i in range(N_BLOCK)]
    other = [other_ref[rows * i : rows * (i + 1)] for i in range(N_BLOCK)]
    above = [jnp.where(upper, a, b) for a, b in zip(mine, other)]
    below = [jnp.where(upper, b, a) for a, b in zip(mine, other)]
    start = (place // (2 * size) * 2 + 1) * size * own
    rate = conductance(
        below[7] - above[8],
        thick_ref[pl.ds(start - 1, 1)],
        thick_ref[pl.ds(start, 1)],
        wet_ref[...] > start,
    )
    rate = rate / (1.0 + rate * (below[0] + above[2]))
    by_forward = rate * (below[3] - above[4])
    by_adjoint = rate * (below[5] - above[6])
    by_top = -rate * above[1]
    by_bottom = rate * below[1]
    flux_ref[0] = by_forward
    flux_ref[1] = by_adjoint
    flux_ref[2] = by_top
    flux_ref[3] = by_bottom
    spread = above[11] - below[10]
    merged = [
        above[0] + above[1] * by_top,
        -below[1] * by_top,
        below[2] - below[1] * by_bottom,
        above[3] + above[1] * by_forward,
        below[4] - below[1] * by_forward,
        above[5] + above[1] * by_adjoint,
        below[6] - below[1] * by_adjoint,
        above[7],
        below[8],
        above[9] + below[9] + by_adjoint * spread,
        above[10] + by_top * spread,
        below[11] + by_bottom * spread,
    ]
    if final:
        upper_next = lax.rem(place // (2 * size), 2) == 0
        merged = last_fields(upper_next, merged)
    for i, field in enumerate(merged):
        block_ref[rows * i : rows * (i + 1)] = field


def last_fields(upper, block):
    return [
        jnp.where(upper, block[2], block[0]),
        jnp.where(upper, block[4], block[3]),
        jnp.where(upper, block[6], block[5]),
        jnp.where(upper, block[8], block[7]),
        block[9],
        jnp.where(upper, block[11], block[10]),
    ]


def final_kernel(
    sizes, own, thick_ref, wet_ref, weight_ref, mine_ref, other_ref, edges_ref, damping_ref, *rest
):
    flux_refs, message_ref, ends_ref = rest[:-2], rest[-2], rest[-1]
    rows, width = wet_ref.shape
    place = lax.axis_index("lev")
    size = sizes[-1]
    upper = lax.rem(place // size, 2) == 0
    start = (place // (2 * size) * 2 + 1) * size * own
    mine = [mine_ref[rows * i : rows * (i + 1)] for i in range(N_LAST)]
    other = [other_ref[rows * i : rows * (i + 1)] for i in range(N_LAST)]
    rate = conductance(
        mine[3] - other[3],
        thick_ref[pl.ds(start - 1, 1)],
        thick_ref[pl.ds(start, 1)],
        wet_ref[...] > start,
    )
    rate = rate / (1.0 + rate * (mine[0] + other[0]))
    in_forward = rate * (other[1] - mine[1])
    in_adjoint = rate * (other[2] - mine[2])
    message_ref[:rows] = mine[4] + other[4] + in_adjoint * (mine[5] - other[5])
    message_ref[rows + 8 :] = damping_ref[...]
    for into, index in ((in_forward, 0), (in_adjoint, 1)):
        top = jnp.where(upper, 0.0, into)
        bottom = jnp.where(upper, into, 0.0)
        for step in range(len(sizes) - 2, -1, -1):
            flux_ref = flux_refs[step]
            flux = flux_ref[index] + top * flux_ref[2] + bottom * flux_ref[3]
            above = lax.rem(place // sizes[step], 2) == 0
            top, bottom = jnp.where(above, top, -flux), jnp.where(above, flux, bottom)
        ends_ref[2 * index] = top
        ends_ref[2 * index + 1] = bottom

    mixed = edges_ref[:8] + edges_ref[8:16] * fold_surface(top) + edges_ref[16:] * fold_surface(bottom)
    message_ref[rows : rows + 8] = weight_ref[...] * mixed


def rest_kernel(
    thick_ref, wet_ref, ends_ref, forward_ref, adjoint_ref, top_ref, bottom_ref, zonal_ref, merid_ref, factor_ref,
    next_tracer_ref, inner_ref,
):
    own, rows, width = forward_ref.shape
    first = lax.axis_index("lev") * own
    lane = lanes(rows, width)
    wet_levels = wet_ref[...]
    ends = [ends_ref[i] for i in range(4)]
    factor = factor_ref[...]
    for k in range(own):
        next_tracer_ref[k] = forward_ref[k] + top_ref[k] * ends[0] + bottom_ref[k] * ends[1]
        mixed = adjoint_ref[k] + top_ref[k] * ends[2] + bottom_ref[k] * ends[3]
        pulled = jnp.where(wet_levels > first + k, thick_ref[pl.ds(first + k, 1)] * mixed, 0.0)
        b_west = jnp.where(lane == 0, 0.0, turn(pulled, 1, 1))
        b_east = jnp.where(lane == width - 1, 0.0, turn(pulled, -1, 1))
        zonal = HALF_STEP * zonal_ref[k]
        u_next = jnp.where(lane == width - 1, spread_edges(factor, rows, k), turn(zonal, -1, 1))
        across = zonal * (pulled - b_west) + u_next * (b_east - pulled)
        step = HALF_STEP * merid_ref[k] * (pulled - turn(pulled, 1, 0))
        inner_ref[k] = pulled + across + step + turn(step, -1, 0)


def total(field):
    while field.ndim > 2:
        field = jnp.sum(field, axis=0)
    return jnp.sum(jnp.sum(field, axis=0, keepdims=True), axis=1, keepdims=True)


def away_order(count):
    return [0, 1, 3, 2] if count == 4 else list(range(count))


def surface_kernel(
    gathered_ref, inner_ref, factor_ref, tracer_adjoint_ref, surface_ref,
    source_scr, damping_scr, edges_scr,
):
    own, rows, width = inner_ref.shape
    count = gathered_ref.shape[0]
    place = lax.axis_index("sub")
    for i, away in enumerate(away_order(count)):
        owner = jnp.bitwise_xor(place, away)
        source_scr[owner] = gathered_ref[i, :rows]
        damping_scr[owner] = gathered_ref[i, rows + 8 :]
        edges_scr[owner] = gathered_ref[i, rows : rows + 8]
    west_edges = edges_scr[lax.rem(place + count - 1, count)]
    east_edges = edges_scr[lax.rem(place + 1, count)]
    beside = factor_ref[...] * beside_edges(west_edges, east_edges)
    lane = lanes(rows, width)
    at_edge = jnp.logical_or(lane == 0, lane == width - 1)
    for k in range(own):
        tracer_adjoint_ref[k] = inner_ref[k] + jnp.where(at_edge, spread_edges(beside, rows, k), 0.0)

    first_lane = lax.broadcasted_iota(jnp.int32, (count, rows, width), 2) == 0
    last_lane = lax.broadcasted_iota(jnp.int32, (count, rows, width), 2) == width - 1
    damping = 4.0 + damping_scr[...]

    def passed(field, shift):
        return jnp.concatenate([field[-shift:], field[:-shift]]) if count > 1 else field

    def image_of(field):
        west = turn(field, 1, 2)
        west = jnp.where(first_lane, passed(west, 1), west)
        east = turn(field, -1, 2)
        east = jnp.where(last_lane, passed(east, -1), east)
        return damping * field - (west + east + turn(field, 1, 1) + turn(field, -1, 1))

    residual = source_scr[...]
    image = image_of(residual)
    norm = total(residual * residual)
    step_size = norm / total(residual * image)
    direction, along = residual, image
    surface = jnp.zeros_like(residual)
    for sweep in range(ITERS):
        surface = surface + step_size * direction
        if sweep + 1 < ITERS:
            residual = residual - step_size * along
            image = image_of(residual)
            norm_next = total(residual * residual)
            product = total(residual * image)
            growth = norm_next / norm
            step_size = norm_next / (product - growth * norm_next / step_size)
            direction = residual + growth * direction
            along = image + growth * along
            norm = norm_next
    source_scr[...] = surface
    surface_ref[...] = source_scr[place]


def on_device(tracer, zonal_flow, meridional_flow, cotangent, thickness, wet_levels):
    own, rows, width = tracer.shape
    lev_count = lax.axis_size("lev")
    sub_count = lax.axis_size("sub")
    edge = in_vmem(rows, width)
    levels = in_vmem(own, rows, width)
    marks = pltpu.VMEM((rows, width), jnp.int32)
    thickness = pltpu.with_memory_space_constraint(thickness, pltpu.SMEM)

    tracer, zonal_flow, wet_levels, east, west, edges = pl.pallas_call(
        pack_kernel,
        out_shape=(levels, levels, marks, in_vmem(16, width), in_vmem(16, width), in_vmem(16, width)),
        in_specs=[pl.BlockSpec(memory_space=pl.ANY)] * 3,
        out_specs=(VMEM_IN,) * 6,
        scratch_shapes=[pltpu.SemaphoreType.DMA((3,))],
        name="pack",
    )(tracer, zonal_flow, wet_levels)
    ring = [(i, (i + 1) % sub_count) for i in range(sub_count)]
    from_west = lax.ppermute(east, "sub", ring)
    from_east = lax.ppermute(west, "sub", [(b, a) for a, b in ring])
    thickness, damping, weights, inside = pl.pallas_call(
        functools.partial(prepare_kernel, own),
        out_shape=(in_vmem(thickness.shape[0], width), edge, in_vmem(8, width), levels),
        in_specs=[SMEM_IN] + [VMEM_IN] * 4,
        out_specs=(VMEM_IN,) * 4,
        name="prepare",
    )(thickness, *near(wet_levels, tracer, zonal_flow, meridional_flow))

    block, forward, adjoint, top, bottom, factor = pl.pallas_call(
        local_kernel,
        out_shape=(in_vmem(N_BLOCK * rows, width), levels, levels, levels, levels, in_vmem(8, width)),
        in_specs=[VMEM_IN] * 8,
        out_specs=(VMEM_IN,) * 6,
        name="local",
    )(*near(thickness, wet_levels, weights, inside, cotangent, edges, from_west, from_east))
    edges = pl.pallas_call(
        edges_kernel, out_shape=in_vmem(24, width), in_specs=[VMEM_IN] * 3, out_specs=VMEM_IN, name="edges"
    )(*near(adjoint, top, bottom))

    sizes = [1]
    while sizes[-1] * 2 < lev_count:
        sizes.append(sizes[-1] * 2)
    fluxes = []
    for size in sizes:
        other = lax.ppermute(block, "lev", [(i, i ^ size) for i in range(lev_count)])
        if size == sizes[-1]:
            break
        final = size * 2 == sizes[-1]
        block, flux = pl.pallas_call(
            functools.partial(merge_kernel, size, final, own),
            out_shape=(in_vmem((N_LAST if final else N_BLOCK) * rows, width), in_vmem(4, rows, width)),
            in_specs=[VMEM_IN] * 4,
            out_specs=(VMEM_IN,) * 2,
            name="merge",
        )(*near(thickness, wet_levels, block, other))
        fluxes.append(flux)

    message, ends = pl.pallas_call(
        functools.partial(final_kernel, sizes, own),
        out_shape=(in_vmem(2 * rows + 8, width), in_vmem(4, rows, width)),
        in_specs=[VMEM_IN] * (7 + len(fluxes)),
        out_specs=(VMEM_IN,) * 2,
        name="final",
    )(*near(thickness, wet_levels, weights, block, other, edges, damping, *fluxes))

    aways = away_order(sub_count)
    if sub_count <= 4:
        gathered = jnp.stack(
            [message]
            + [lax.ppermute(message, "sub", [(i, i ^ away) for i in range(sub_count)]) for away in aways[1:]]
        )
    else:
        gathered = message[None]
        while gathered.shape[0] < sub_count:
            size = gathered.shape[0]
            got = lax.ppermute(gathered, "sub", [(i, i ^ size) for i in range(sub_count)])
            gathered = jnp.concatenate([gathered, got])

    next_tracer, inner = pl.pallas_call(
        rest_kernel,
        out_shape=(jax.ShapeDtypeStruct(tracer.shape, jnp.float32), levels),
        in_specs=[VMEM_IN] * 10,
        out_specs=(VMEM_IN,) * 2,
        name="rest",
    )(*near(thickness, wet_levels, ends, forward, adjoint, top, bottom, zonal_flow, meridional_flow, factor))

    tracer_adjoint, surface = pl.pallas_call(
        surface_kernel,
        out_shape=(
            jax.ShapeDtypeStruct(tracer.shape, jnp.float32),
            jax.ShapeDtypeStruct((rows, width), jnp.float32),
        ),
        in_specs=[VMEM_IN] * 3,
        out_specs=(VMEM_IN,) * 2,
        scratch_shapes=[pltpu.VMEM((sub_count, rows, width), jnp.float32)] * 2
        + [pltpu.VMEM((sub_count, 8, width), jnp.float32)],
        name="surface",
    )(*near(gathered, inner, factor))
    return (next_tracer, tracer_adjoint, surface)


def solution(mesh):
    whole = P(("members", "lev"), None, "sub")
    return jax.shard_map(
        on_device,
        mesh=mesh,
        in_specs=(whole, whole, whole, whole, P(), P(None, "sub")),
        out_specs=(whole, whole, P("members", "sub")),
        check_vma=False,
    )
```

```python
import functools

import jax
import jax.numpy as jnp
from jax import lax
from jax.experimental import pallas as pl
from jax.experimental.pallas import tpu as pltpu
from jax.sharding import PartitionSpec as P

ITERS = 3
ADVECT_STEP = 0.25
MIX_RATE = 2.0
HALF_STEP = 0.5 * ADVECT_STEP

N_BLOCK = 12
N_LAST = 6

VMEM_IN = pl.BlockSpec(memory_space=pltpu.VMEM)
SMEM_IN = pl.BlockSpec(memory_space=pltpu.SMEM)


def in_vmem(*shape):
    return pltpu.VMEM(shape, jnp.float32)


def near(*arrays):
    return [pltpu.with_memory_space_constraint(array, pltpu.VMEM) for array in arrays]


def lanes(rows, width):
    return lax.broadcasted_iota(jnp.int32, (rows, width), 1)


def turn(field, shift, axis):
    size = field.shape[axis]
    shift = shift % size
    return field if shift == 0 else pltpu.roll(field, shift, axis)


def splat(scalar, width):
    return jnp.full((1, width), scalar, jnp.float32)


def conductance(drop, upper_thick, lower_thick, wet):
    spacing = 0.5 * (upper_thick + lower_thick)
    rate = 0.2 / spacing + spacing / (spacing * spacing + drop * drop)
    return jnp.where(wet, MIX_RATE * rate, 0.0)


def parity(width):
    return lax.rem(lanes(8, width), 2)


def fold_edges(levels):
    rows, width = levels[0].shape
    groups = rows // 8
    slot = width // groups
    pair = lanes(8, width) // 2
    folded = jnp.zeros((8, width), levels[0].dtype)
    for k, field in enumerate(levels):
        for group in range(groups):
            place = slot * group + 2 * k
            turned = turn(field[8 * group : 8 * group + 8], place + 1, 1)
            folded = jnp.where(pair == place // 2, turned, folded)
    return folded


def fold_surface(field):
    rows, width = field.shape
    groups = rows // 8
    slot = width // groups
    group_of = lanes(8, width) // slot
    folded = jnp.zeros((8, width), field.dtype)
    for group in range(groups):
        part = field[8 * group : 8 * group + 8]
        ends = jnp.where(
            parity(width) == 0,
            jnp.broadcast_to(part[:, width - 1 :], part.shape),
            jnp.broadcast_to(part[:, :1], part.shape),
        )
        folded = jnp.where(group_of == group, ends, folded)
    return folded


def beside_edges(from_west, from_east):
    return jnp.where(parity(from_west.shape[1]) == 0, turn(from_east, -1, 1), turn(from_west, 1, 1))


def spread_edges(beside, rows, k):
    width = beside.shape[1]
    groups = rows // 8
    slot = width // groups
    return jnp.concatenate([turn(beside, -(slot * group + 2 * k + 1), 1) for group in range(groups)])


def pack_kernel(
    tracer_hbm, zonal_hbm, wet_hbm, tracer_ref, zonal_ref, wet_ref, east_ref, west_ref, edges_ref, sems
):
    own = tracer_ref.shape[0]
    copies = [
        pltpu.make_async_copy(source, target, sems.at[i])
        for i, (source, target) in enumerate(
            ((tracer_hbm, tracer_ref), (zonal_hbm, zonal_ref), (wet_hbm, wet_ref))
        )
    ]
    for copy in copies:
        copy.start()
    copies[0].wait()
    east = fold_edges([tracer_ref[k] for k in range(own)])
    copies[1].wait()
    zonal = fold_edges([zonal_ref[k] for k in range(own)])
    for ref in (east_ref, west_ref, edges_ref):
        ref[:8] = east
        ref[8:] = zonal
    copies[2].wait()


def prepare_kernel(
    own, thick_ref, wet_ref, tracer_ref, zonal_ref, merid_ref, rows_ref, damping_ref, weight_ref, inside_ref
):
    level_count = thick_ref.shape[0]
    rows, width = wet_ref.shape
    wet_levels = wet_ref[...]
    depth = jnp.zeros((rows, width), jnp.float32)
    for k in range(level_count):
        thick = splat(thick_ref[k], width)
        rows_ref[k : k + 1] = thick
        depth = depth + jnp.where(wet_levels > k, thick, 0.0)
    damping_ref[...] = 0.3 + depth / level_count
    wet_edges = fold_surface(wet_levels)
    offset = lax.rem(lanes(8, width), width // (rows // 8)) // 2
    place = lax.axis_index("lev")
    for i in range(2):
        first = (place // 2 * 2 + i) * own
        thick = jnp.zeros((8, width), jnp.float32)
        for k in range(own):
            thick = jnp.where(offset == k, thick_ref[first + k], thick)
        weight_ref[8 * i : 8 * i + 8] = jnp.where(wet_edges > offset + first, thick, 0.0)
    first = place * own
    lane = lanes(rows, width)
    for k in range(own):
        values = tracer_ref[k]
        zonal = zonal_ref[k]
        c_west = jnp.where(lane == 0, 0.0, turn(values, 1, 1))
        u_next = jnp.where(lane == width - 1, 0.0, turn(zonal, -1, 1))
        flux_y = merid_ref[k] * (turn(values, 1, 0) + values)
        change = u_next * (values + turn(values, -1, 1)) - zonal * (c_west + values) + (turn(flux_y, -1, 0) - flux_y)
        inside_ref[k] = jnp.where(wet_levels > first + k, values - HALF_STEP * change, 0.0)


def local_kernel(
    thick_ref, wet_ref, weight_ref, inside_ref, cot_ref, edges_ref, from_west_ref, from_east_ref,
    block_ref, forward_ref, adjoint_ref, top_ref, bottom_ref, factor_ref,
):
    own, rows, width = cot_ref.shape
    first = lax.axis_index("lev") * own
    lane = lanes(rows, width)
    at_edge = jnp.logical_or(lane == 0, lane == width - 1)
    even = parity(width) == 0
    wet_levels = wet_ref[...]
    factor = HALF_STEP * jnp.where(even, turn(from_east_ref[8:], -1, 1), -edges_ref[8:])
    factor_ref[...] = factor
    beside = beside_edges(from_west_ref[:8], from_east_ref[:8])
    beside = -factor * jnp.where(even, edges_ref[:8] + beside, beside)
    weight = jnp.where(lax.rem(lax.axis_index("lev"), 2) == 0, weight_ref[:8], weight_ref[8:])
    beside = jnp.where(weight > 0.0, beside, 0.0)
    forward = []
    for k in range(own):
        forward.append(inside_ref[k] + jnp.where(at_edge, spread_edges(beside, rows, k), 0.0))

    thick = [thick_ref[pl.ds(first + k, 1)] for k in range(own)]
    conduct = [None]
    for k in range(1, own):
        conduct.append(
            conductance(forward[k] - forward[k - 1], thick[k - 1], thick[k], wet_levels > first + k)
        )
    pivot = jnp.broadcast_to(thick[0], (rows, width))
    ratio, scale = [None], []
    g_forward = [thick[0] * forward[0]]
    g_adjoint = [cot_ref[0]]
    g_top = [jnp.ones((rows, width), jnp.float32)]
    for k in range(1, own):
        inverse = 1.0 / (pivot + conduct[k])
        scale.append(inverse)
        ratio.append(conduct[k] * inverse)
        pivot = thick[k] + pivot * ratio[k]
        g_forward.append(thick[k] * forward[k] + ratio[k] * g_forward[k - 1])
        g_adjoint.append(cot_ref[k] + ratio[k] * g_adjoint[k - 1])
        g_top.append(ratio[k] * g_top[k - 1])
    scale.append(1.0 / pivot)

    def put(index, field):
        block_ref[rows * index : rows * (index + 1)] = field

    last = own - 1
    y_forward = g_forward[last] * scale[last]
    y_adjoint = g_adjoint[last] * scale[last]
    y_top = g_top[last] * scale[last]
    y_bottom = scale[last]
    put(1, y_top)
    put(2, y_bottom)
    put(4, y_forward)
    put(6, y_adjoint)
    put(7, forward[0])
    put(8, forward[last])
    sums = [jnp.zeros((rows, width), jnp.float32)] * 3
    for k in range(last, -1, -1):
        if k < last:
            y_forward = g_forward[k] * scale[k] + ratio[k + 1] * y_forward
            y_adjoint = g_adjoint[k] * scale[k] + ratio[k + 1] * y_adjoint
            y_top = g_top[k] * scale[k] + ratio[k + 1] * y_top
            y_bottom = ratio[k + 1] * y_bottom
        forward_ref[k] = y_forward
        adjoint_ref[k] = y_adjoint
        top_ref[k] = y_top
        bottom_ref[k] = y_bottom
        square = thick[k] * thick[k]
        sums = [s + square * y for s, y in zip(sums, (y_adjoint, y_top, y_bottom))]
    put(0, y_top)
    put(3, y_forward)
    put(5, y_adjoint)
    for i in range(3):
        put(9 + i, sums[i])


def edges_kernel(adjoint_ref, top_ref, bottom_ref, edges_ref):
    for i, ref in enumerate((adjoint_ref, top_ref, bottom_ref)):
        edges_ref[8 * i : 8 * i + 8] = fold_edges([ref[k] for k in range(ref.shape[0])])


def merge_kernel(size, final, own, thick_ref, wet_ref, mine_ref, other_ref, block_ref, flux_ref):
    place = lax.axis_index("lev")
    rows, width = wet_ref.shape
    upper = lax.rem(place // size, 2) == 0
    mine = [mine_ref[rows * i : rows * (i + 1)] for i in range(N_BLOCK)]
    other = [other_ref[rows * i : rows * (i + 1)] for i in range(N_BLOCK)]
    above = [jnp.where(upper, a, b) for a, b in zip(mine, other)]
    below = [jnp.where(upper, b, a) for a, b in zip(mine, other)]
    start = (place // (2 * size) * 2 + 1) * size * own
    rate = conductance(
        below[7] - above[8],
        thick_ref[pl.ds(start - 1, 1)],
        thick_ref[pl.ds(start, 1)],
        wet_ref[...] > start,
    )
    rate = rate / (1.0 + rate * (below[0] + above[2]))
    by_forward = rate * (below[3] - above[4])
    by_adjoint = rate * (below[5] - above[6])
    by_top = -rate * above[1]
    by_bottom = rate * below[1]
    flux_ref[0] = by_forward
    flux_ref[1] = by_adjoint
    flux_ref[2] = by_top
    flux_ref[3] = by_bottom
    spread = above[11] - below[10]
    merged = [
        above[0] + above[1] * by_top,
        -below[1] * by_top,
        below[2] - below[1] * by_bottom,
        above[3] + above[1] * by_forward,
        below[4] - below[1] * by_forward,
        above[5] + above[1] * by_adjoint,
        below[6] - below[1] * by_adjoint,
        above[7],
        below[8],
        above[9] + below[9] + by_adjoint * spread,
        above[10] + by_top * spread,
        below[11] + by_bottom * spread,
    ]
    if final:
        upper_next = lax.rem(place // (2 * size), 2) == 0
        merged = last_fields(upper_next, merged)
    for i, field in enumerate(merged):
        block_ref[rows * i : rows * (i + 1)] = field


def last_fields(upper, block):
    return [
        jnp.where(upper, block[2], block[0]),
        jnp.where(upper, block[4], block[3]),
        jnp.where(upper, block[6], block[5]),
        jnp.where(upper, block[8], block[7]),
        block[9],
        jnp.where(upper, block[11], block[10]),
    ]


def final_kernel(
    sizes, own, thick_ref, wet_ref, weight_ref, mine_ref, other_ref, edges_ref, other_edges_ref, damping_ref, *rest
):
    flux_refs, message_ref, ends_ref = rest[:-2], rest[-2], rest[-1]
    rows, width = wet_ref.shape
    place = lax.axis_index("lev")
    size = sizes[-1]
    upper = lax.rem(place // size, 2) == 0
    start = (place // (2 * size) * 2 + 1) * size * own
    mine = [mine_ref[rows * i : rows * (i + 1)] for i in range(N_LAST)]
    other = [other_ref[rows * i : rows * (i + 1)] for i in range(N_LAST)]
    rate = conductance(
        mine[3] - other[3],
        thick_ref[pl.ds(start - 1, 1)],
        thick_ref[pl.ds(start, 1)],
        wet_ref[...] > start,
    )
    rate = rate / (1.0 + rate * (mine[0] + other[0]))
    in_forward = rate * (other[1] - mine[1])
    in_adjoint = rate * (other[2] - mine[2])
    message_ref[:rows] = mine[4] + other[4] + in_adjoint * (mine[5] - other[5])
    message_ref[rows + 16 :] = damping_ref[...]
    even = lax.rem(place, 2) == 0
    pair = []
    for into, index in ((in_forward, 0), (in_adjoint, 1)):
        top = jnp.where(upper, 0.0, into)
        bottom = jnp.where(upper, into, 0.0)
        for step in range(len(sizes) - 2, -1, -1):
            flux_ref = flux_refs[step]
            flux = flux_ref[index] + top * flux_ref[2] + bottom * flux_ref[3]
            if step == 0:
                pair = [(top, flux), (-flux, bottom)]
            above = lax.rem(place // sizes[step], 2) == 0
            top, bottom = jnp.where(above, top, -flux), jnp.where(above, flux, bottom)
        ends_ref[2 * index] = top
        ends_ref[2 * index + 1] = bottom
    for i, (top, bottom) in enumerate(pair):
        is_mine = even if i == 0 else jnp.logical_not(even)
        edges = jnp.where(is_mine, edges_ref[...], other_edges_ref[...])
        mixed = edges[:8] + edges[8:16] * fold_surface(top) + edges[16:] * fold_surface(bottom)
        message_ref[rows + 8 * i : rows + 8 * i + 8] = weight_ref[8 * i : 8 * i + 8] * mixed


def rest_kernel(
    thick_ref, wet_ref, ends_ref, forward_ref, adjoint_ref, top_ref, bottom_ref, zonal_ref, merid_ref, factor_ref,
    next_tracer_ref, inner_ref,
):
    own, rows, width = forward_ref.shape
    first = lax.axis_index("lev") * own
    lane = lanes(rows, width)
    wet_levels = wet_ref[...]
    ends = [ends_ref[i] for i in range(4)]
    factor = factor_ref[...]
    for k in range(own):
        next_tracer_ref[k] = forward_ref[k] + top_ref[k] * ends[0] + bottom_ref[k] * ends[1]
        mixed = adjoint_ref[k] + top_ref[k] * ends[2] + bottom_ref[k] * ends[3]
        pulled = jnp.where(wet_levels > first + k, thick_ref[pl.ds(first + k, 1)] * mixed, 0.0)
        b_west = jnp.where(lane == 0, 0.0, turn(pulled, 1, 1))
        b_east = jnp.where(lane == width - 1, 0.0, turn(pulled, -1, 1))
        zonal = HALF_STEP * zonal_ref[k]
        u_next = jnp.where(lane == width - 1, spread_edges(factor, rows, k), turn(zonal, -1, 1))
        across = zonal * (pulled - b_west) + u_next * (b_east - pulled)
        step = HALF_STEP * merid_ref[k] * (pulled - turn(pulled, 1, 0))
        inner_ref[k] = pulled + across + step + turn(step, -1, 0)


def total(field):
    while field.ndim > 2:
        field = jnp.sum(field, axis=0)
    return jnp.sum(jnp.sum(field, axis=0, keepdims=True), axis=1, keepdims=True)


def routes(count):
    if count == 4:
        return [[2, 3, 1, 0], [3, 2, 0, 1], [1, 0, 3, 2]]
    return [[i ^ away for i in range(count)] for away in range(1, count)]


def crossed(route, lev_count):
    return [(s * lev_count + l, t * lev_count + (l ^ 1)) for s, t in enumerate(route) for l in range(lev_count)]


def owner_of(route, place):
    owner = 0
    for source, target in enumerate(route):
        owner = jnp.where(place == target, source, owner)
    return owner


def surface_kernel(
    gathered_ref, inner_ref, factor_ref, tracer_adjoint_ref, surface_ref,
    source_scr, damping_scr, edges_scr,
):
    own, rows, width = inner_ref.shape
    count = gathered_ref.shape[0]
    place = lax.axis_index("sub")
    even = lax.rem(lax.axis_index("lev"), 2) == 0
    ways = [list(range(count))] + routes(count)[:: -1 if count == 4 else 1]
    for i, route in enumerate(ways):
        owner = owner_of(route, place)
        source_scr[owner] = gathered_ref[i, :rows]
        damping_scr[owner] = gathered_ref[i, rows + 16 :]
        edges_scr[owner] = jnp.where(even, gathered_ref[i, rows : rows + 8], gathered_ref[i, rows + 8 : rows + 16])
    west_edges = edges_scr[lax.rem(place + count - 1, count)]
    east_edges = edges_scr[lax.rem(place + 1, count)]
    beside = factor_ref[...] * beside_edges(west_edges, east_edges)
    lane = lanes(rows, width)
    at_edge = jnp.logical_or(lane == 0, lane == width - 1)
    for k in range(own):
        tracer_adjoint_ref[k] = inner_ref[k] + jnp.where(at_edge, spread_edges(beside, rows, k), 0.0)

    first_lane = lax.broadcasted_iota(jnp.int32, (count, rows, width), 2) == 0
    last_lane = lax.broadcasted_iota(jnp.int32, (count, rows, width), 2) == width - 1
    damping = 4.0 + damping_scr[...]

    def passed(field, shift):
        return jnp.concatenate([field[-shift:], field[:-shift]]) if count > 1 else field

    def image_of(field):
        west = turn(field, 1, 2)
        west = jnp.where(first_lane, passed(west, 1), west)
        east = turn(field, -1, 2)
        east = jnp.where(last_lane, passed(east, -1), east)
        return damping * field - (west + east + turn(field, 1, 1) + turn(field, -1, 1))

    residual = source_scr[...]
    image = image_of(residual)
    norm = total(residual * residual)
    step_size = norm / total(residual * image)
    direction, along = residual, image
    surface = jnp.zeros_like(residual)
    for sweep in range(ITERS):
        surface = surface + step_size * direction
        if sweep + 1 < ITERS:
            residual = residual - step_size * along
            image = image_of(residual)
            norm_next = total(residual * residual)
            product = total(residual * image)
            growth = norm_next / norm
            step_size = norm_next / (product - growth * norm_next / step_size)
            direction = residual + growth * direction
            along = image + growth * along
            norm = norm_next
    source_scr[...] = surface
    surface_ref[...] = source_scr[place]


def on_device(tracer, zonal_flow, meridional_flow, cotangent, thickness, wet_levels):
    own, rows, width = tracer.shape
    lev_count = lax.axis_size("lev")
    sub_count = lax.axis_size("sub")
    edge = in_vmem(rows, width)
    levels = in_vmem(own, rows, width)
    marks = pltpu.VMEM((rows, width), jnp.int32)
    thickness = pltpu.with_memory_space_constraint(thickness, pltpu.SMEM)

    tracer, zonal_flow, wet_levels, east, west, edges = pl.pallas_call(
        pack_kernel,
        out_shape=(levels, levels, marks, in_vmem(16, width), in_vmem(16, width), in_vmem(16, width)),
        in_specs=[pl.BlockSpec(memory_space=pl.ANY)] * 3,
        out_specs=(VMEM_IN,) * 6,
        scratch_shapes=[pltpu.SemaphoreType.DMA((3,))],
        name="pack",
    )(tracer, zonal_flow, wet_levels)
    ring = [(i, (i + 1) % sub_count) for i in range(sub_count)]
    from_west = lax.ppermute(east, "sub", ring)
    from_east = lax.ppermute(west, "sub", [(b, a) for a, b in ring])
    thickness, damping, weights, inside = pl.pallas_call(
        functools.partial(prepare_kernel, own),
        out_shape=(in_vmem(thickness.shape[0], width), edge, in_vmem(16, width), levels),
        in_specs=[SMEM_IN] + [VMEM_IN] * 4,
        out_specs=(VMEM_IN,) * 4,
        name="prepare",
    )(thickness, *near(wet_levels, tracer, zonal_flow, meridional_flow))

    block, forward, adjoint, top, bottom, factor = pl.pallas_call(
        local_kernel,
        out_shape=(in_vmem(N_BLOCK * rows, width), levels, levels, levels, levels, in_vmem(8, width)),
        in_specs=[VMEM_IN] * 8,
        out_specs=(VMEM_IN,) * 6,
        name="local",
    )(*near(thickness, wet_levels, weights, inside, cotangent, edges, from_west, from_east))
    edges = pl.pallas_call(
        edges_kernel, out_shape=in_vmem(24, width), in_specs=[VMEM_IN] * 3, out_specs=VMEM_IN, name="edges"
    )(*near(adjoint, top, bottom))
    other_edges = lax.ppermute(edges, "lev", [(i, i ^ 1) for i in range(lev_count)])

    sizes = [1]
    while sizes[-1] * 2 < lev_count:
        sizes.append(sizes[-1] * 2)
    fluxes = []
    for size in sizes:
        other = lax.ppermute(block, "lev", [(i, i ^ (2 * size - 1)) for i in range(lev_count)])
        if size == sizes[-1]:
            break
        final = size * 2 == sizes[-1]
        block, flux = pl.pallas_call(
            functools.partial(merge_kernel, size, final, own),
            out_shape=(in_vmem((N_LAST if final else N_BLOCK) * rows, width), in_vmem(4, rows, width)),
            in_specs=[VMEM_IN] * 4,
            out_specs=(VMEM_IN,) * 2,
            name="merge",
        )(*near(thickness, wet_levels, block, other))
        fluxes.append(flux)

    message, ends = pl.pallas_call(
        functools.partial(final_kernel, sizes, own),
        out_shape=(in_vmem(2 * rows + 16, width), in_vmem(4, rows, width)),
        in_specs=[VMEM_IN] * (8 + len(fluxes)),
        out_specs=(VMEM_IN,) * 2,
        name="final",
    )(*near(thickness, wet_levels, weights, block, other, edges, other_edges, damping, *fluxes))

    if sub_count == 4:
        gathered = jnp.stack(
            [message] + [lax.ppermute(message, ("sub", "lev"), crossed(way, lev_count)) for way in routes(sub_count)[::-1]]
        )
    else:
        gathered = message[None]
        while gathered.shape[0] < sub_count:
            size = gathered.shape[0]
            got = lax.ppermute(gathered, "sub", [(i, i ^ size) for i in range(sub_count)])
            gathered = jnp.concatenate([gathered, got])

    next_tracer, inner = pl.pallas_call(
        rest_kernel,
        out_shape=(jax.ShapeDtypeStruct(tracer.shape, jnp.float32), levels),
        in_specs=[VMEM_IN] * 10,
        out_specs=(VMEM_IN,) * 2,
        name="rest",
    )(*near(thickness, wet_levels, ends, forward, adjoint, top, bottom, zonal_flow, meridional_flow, factor))

    tracer_adjoint, surface = pl.pallas_call(
        surface_kernel,
        out_shape=(
            jax.ShapeDtypeStruct(tracer.shape, jnp.float32),
            jax.ShapeDtypeStruct((rows, width), jnp.float32),
        ),
        in_specs=[VMEM_IN] * 3,
        out_specs=(VMEM_IN,) * 2,
        scratch_shapes=[pltpu.VMEM((sub_count, rows, width), jnp.float32)] * 2
        + [pltpu.VMEM((sub_count, 8, width), jnp.float32)],
        name="surface",
    )(*near(gathered, inner, factor))
    return (next_tracer, tracer_adjoint, surface)


def solution(mesh):
    whole = P(("members", "lev"), None, "sub")
    return jax.shard_map(
        on_device,
        mesh=mesh,
        in_specs=(whole, whole, whole, whole, P(), P(None, "sub")),
        out_specs=(whole, whole, P("members", "sub")),
        check_vma=False,
    )
```

```python
import functools

import jax
import jax.numpy as jnp
from jax import lax
from jax.experimental import pallas as pl
from jax.experimental.pallas import tpu as pltpu
from jax.sharding import PartitionSpec as P

ITERS = 3
ADVECT_STEP = 0.25
MIX_RATE = 2.0
HALF_STEP = 0.5 * ADVECT_STEP

N_BLOCK = 12
N_LAST = 6

VMEM_IN = pl.BlockSpec(memory_space=pltpu.VMEM)
SMEM_IN = pl.BlockSpec(memory_space=pltpu.SMEM)


def in_vmem(*shape):
    return pltpu.VMEM(shape, jnp.float32)


def near(*arrays):
    return [pltpu.with_memory_space_constraint(array, pltpu.VMEM) for array in arrays]


def lanes(rows, width):
    return lax.broadcasted_iota(jnp.int32, (rows, width), 1)


def turn(field, shift, axis):
    size = field.shape[axis]
    shift = shift % size
    return field if shift == 0 else pltpu.roll(field, shift, axis)


def splat(scalar, width):
    return jnp.full((1, width), scalar, jnp.float32)


def conductance(drop, upper_thick, lower_thick, wet):
    spacing = 0.5 * (upper_thick + lower_thick)
    rate = 0.2 / spacing + spacing / (spacing * spacing + drop * drop)
    return jnp.where(wet, MIX_RATE * rate, 0.0)


def parity(width):
    return lax.rem(lanes(8, width), 2)


def fold_edges(levels):
    rows, width = levels[0].shape
    groups = rows // 8
    slot = width // groups
    pair = lanes(8, width) // 2
    folded = jnp.zeros((8, width), levels[0].dtype)
    for k, field in enumerate(levels):
        for group in range(groups):
            place = slot * group + 2 * k
            turned = turn(field[8 * group : 8 * group + 8], place + 1, 1)
            folded = jnp.where(pair == place // 2, turned, folded)
    return folded


def fold_surface(field):
    rows, width = field.shape
    groups = rows // 8
    slot = width // groups
    group_of = lanes(8, width) // slot
    folded = jnp.zeros((8, width), field.dtype)
    for group in range(groups):
        part = field[8 * group : 8 * group + 8]
        ends = jnp.where(
            parity(width) == 0,
            jnp.broadcast_to(part[:, width - 1 :], part.shape),
            jnp.broadcast_to(part[:, :1], part.shape),
        )
        folded = jnp.where(group_of == group, ends, folded)
    return folded


def beside_edges(from_west, from_east):
    return jnp.where(parity(from_west.shape[1]) == 0, turn(from_east, -1, 1), turn(from_west, 1, 1))


def spread_edges(beside, rows, k):
    width = beside.shape[1]
    groups = rows // 8
    slot = width // groups
    return jnp.concatenate([turn(beside, -(slot * group + 2 * k + 1), 1) for group in range(groups)])


def pack_kernel(
    tracer_hbm, zonal_hbm, wet_hbm, tracer_ref, zonal_ref, wet_ref, east_ref, west_ref, edges_ref, sems
):
    own = tracer_ref.shape[0]
    copies = [
        pltpu.make_async_copy(source, target, sems.at[i])
        for i, (source, target) in enumerate(
            ((tracer_hbm, tracer_ref), (zonal_hbm, zonal_ref), (wet_hbm, wet_ref))
        )
    ]
    for copy in copies:
        copy.start()
    copies[0].wait()
    east = fold_edges([tracer_ref[k] for k in range(own)])
    copies[1].wait()
    zonal = fold_edges([zonal_ref[k] for k in range(own)])
    copies[2].wait()
    for ref in (east_ref, west_ref, edges_ref):
        ref[:8] = east
        ref[8:16] = zonal
        ref[16:] = wet_ref[...].astype(jnp.float32)


def damping_of(wet_levels, thick_ref):
    level_count = thick_ref.shape[0]
    depth = jnp.zeros(wet_levels.shape, jnp.float32)
    for k in range(level_count):
        depth = depth + jnp.where(wet_levels > k, thick_ref[k : k + 1], 0.0)
    return 0.3 + depth / level_count


def prepare_kernel(
    own, thick_ref, wet_ref, tracer_ref, zonal_ref, merid_ref, rows_ref, damping_ref, weight_ref, inside_ref
):
    level_count = thick_ref.shape[0]
    rows, width = wet_ref.shape
    wet_levels = wet_ref[...]
    for k in range(level_count):
        rows_ref[k : k + 1] = splat(thick_ref[k], width)
    damping_ref[...] = damping_of(wet_levels, rows_ref)
    wet_edges = fold_surface(wet_levels)
    offset = lax.rem(lanes(8, width), width // (rows // 8)) // 2
    place = lax.axis_index("lev")
    for i in range(2):
        first = (place // 2 * 2 + i) * own
        thick = jnp.zeros((8, width), jnp.float32)
        for k in range(own):
            thick = jnp.where(offset == k, thick_ref[first + k], thick)
        weight_ref[8 * i : 8 * i + 8] = jnp.where(wet_edges > offset + first, thick, 0.0)
    first = place * own
    lane = lanes(rows, width)
    for k in range(own):
        values = tracer_ref[k]
        zonal = zonal_ref[k]
        c_west = jnp.where(lane == 0, 0.0, turn(values, 1, 1))
        u_next = jnp.where(lane == width - 1, 0.0, turn(zonal, -1, 1))
        flux_y = merid_ref[k] * (turn(values, 1, 0) + values)
        change = u_next * (values + turn(values, -1, 1)) - zonal * (c_west + values) + (turn(flux_y, -1, 0) - flux_y)
        inside_ref[k] = jnp.where(wet_levels > first + k, values - HALF_STEP * change, 0.0)


def local_kernel(
    thick_ref, wet_ref, weight_ref, inside_ref, cot_ref, edges_ref, from_west_ref, from_east_ref,
    block_ref, forward_ref, adjoint_ref, top_ref, bottom_ref, factor_ref,
):
    own, rows, width = cot_ref.shape
    first = lax.axis_index("lev") * own
    lane = lanes(rows, width)
    at_edge = jnp.logical_or(lane == 0, lane == width - 1)
    even = parity(width) == 0
    wet_levels = wet_ref[...]
    factor = HALF_STEP * jnp.where(even, turn(from_east_ref[8:16], -1, 1), -edges_ref[8:16])
    factor_ref[...] = factor
    beside = beside_edges(from_west_ref[:8], from_east_ref[:8])
    beside = -factor * jnp.where(even, edges_ref[:8] + beside, beside)
    weight = jnp.where(lax.rem(lax.axis_index("lev"), 2) == 0, weight_ref[:8], weight_ref[8:])
    beside = jnp.where(weight > 0.0, beside, 0.0)
    forward = []
    for k in range(own):
        forward.append(inside_ref[k] + jnp.where(at_edge, spread_edges(beside, rows, k), 0.0))

    thick = [thick_ref[pl.ds(first + k, 1)] for k in range(own)]
    conduct = [None]
    for k in range(1, own):
        conduct.append(
            conductance(forward[k] - forward[k - 1], thick[k - 1], thick[k], wet_levels > first + k)
        )
    pivot = jnp.broadcast_to(thick[0], (rows, width))
    ratio, scale = [None], []
    g_forward = [thick[0] * forward[0]]
    g_adjoint = [cot_ref[0]]
    g_top = [jnp.ones((rows, width), jnp.float32)]
    for k in range(1, own):
        inverse = 1.0 / (pivot + conduct[k])
        scale.append(inverse)
        ratio.append(conduct[k] * inverse)
        pivot = thick[k] + pivot * ratio[k]
        g_forward.append(thick[k] * forward[k] + ratio[k] * g_forward[k - 1])
        g_adjoint.append(cot_ref[k] + ratio[k] * g_adjoint[k - 1])
        g_top.append(ratio[k] * g_top[k - 1])
    scale.append(1.0 / pivot)

    def put(index, field):
        block_ref[rows * index : rows * (index + 1)] = field

    last = own - 1
    y_forward = g_forward[last] * scale[last]
    y_adjoint = g_adjoint[last] * scale[last]
    y_top = g_top[last] * scale[last]
    y_bottom = scale[last]
    put(1, y_top)
    put(2, y_bottom)
    put(4, y_forward)
    put(6, y_adjoint)
    put(7, forward[0])
    put(8, forward[last])
    sums = [jnp.zeros((rows, width), jnp.float32)] * 3
    for k in range(last, -1, -1):
        if k < last:
            y_forward = g_forward[k] * scale[k] + ratio[k + 1] * y_forward
            y_adjoint = g_adjoint[k] * scale[k] + ratio[k + 1] * y_adjoint
            y_top = g_top[k] * scale[k] + ratio[k + 1] * y_top
            y_bottom = ratio[k + 1] * y_bottom
        forward_ref[k] = y_forward
        adjoint_ref[k] = y_adjoint
        top_ref[k] = y_top
        bottom_ref[k] = y_bottom
        square = thick[k] * thick[k]
        sums = [s + square * y for s, y in zip(sums, (y_adjoint, y_top, y_bottom))]
    put(0, y_top)
    put(3, y_forward)
    put(5, y_adjoint)
    for i in range(3):
        put(9 + i, sums[i])


def edges_kernel(adjoint_ref, top_ref, bottom_ref, edges_ref):
    for i, ref in enumerate((adjoint_ref, top_ref, bottom_ref)):
        edges_ref[8 * i : 8 * i + 8] = fold_edges([ref[k] for k in range(ref.shape[0])])


def merge_kernel(size, final, own, thick_ref, wet_ref, mine_ref, other_ref, block_ref, flux_ref):
    place = lax.axis_index("lev")
    rows, width = wet_ref.shape
    upper = lax.rem(place // size, 2) == 0
    mine = [mine_ref[rows * i : rows * (i + 1)] for i in range(N_BLOCK)]
    other = [other_ref[rows * i : rows * (i + 1)] for i in range(N_BLOCK)]
    above = [jnp.where(upper, a, b) for a, b in zip(mine, other)]
    below = [jnp.where(upper, b, a) for a, b in zip(mine, other)]
    start = (place // (2 * size) * 2 + 1) * size * own
    rate = conductance(
        below[7] - above[8],
        thick_ref[pl.ds(start - 1, 1)],
        thick_ref[pl.ds(start, 1)],
        wet_ref[...] > start,
    )
    rate = rate / (1.0 + rate * (below[0] + above[2]))
    by_forward = rate * (below[3] - above[4])
    by_adjoint = rate * (below[5] - above[6])
    by_top = -rate * above[1]
    by_bottom = rate * below[1]
    flux_ref[0] = by_forward
    flux_ref[1] = by_adjoint
    flux_ref[2] = by_top
    flux_ref[3] = by_bottom
    spread = above[11] - below[10]
    merged = [
        above[0] + above[1] * by_top,
        -below[1] * by_top,
        below[2] - below[1] * by_bottom,
        above[3] + above[1] * by_forward,
        below[4] - below[1] * by_forward,
        above[5] + above[1] * by_adjoint,
        below[6] - below[1] * by_adjoint,
        above[7],
        below[8],
        above[9] + below[9] + by_adjoint * spread,
        above[10] + by_top * spread,
        below[11] + by_bottom * spread,
    ]
    if final:
        upper_next = lax.rem(place // (2 * size), 2) == 0
        merged = last_fields(upper_next, merged)
    for i, field in enumerate(merged):
        block_ref[rows * i : rows * (i + 1)] = field


def last_fields(upper, block):
    return [
        jnp.where(upper, block[2], block[0]),
        jnp.where(upper, block[4], block[3]),
        jnp.where(upper, block[6], block[5]),
        jnp.where(upper, block[8], block[7]),
        block[9],
        jnp.where(upper, block[11], block[10]),
    ]


def final_kernel(
    sizes, own, thick_ref, wet_ref, weight_ref, mine_ref, other_ref, edges_ref, damping_ref, *rest
):
    flux_refs, message_ref, ends_ref = rest[:-2], rest[-2], rest[-1]
    rows, width = wet_ref.shape
    place = lax.axis_index("lev")
    size = sizes[-1]
    upper = lax.rem(place // size, 2) == 0
    start = (place // (2 * size) * 2 + 1) * size * own
    mine = [mine_ref[rows * i : rows * (i + 1)] for i in range(N_LAST)]
    other = [other_ref[rows * i : rows * (i + 1)] for i in range(N_LAST)]
    rate = conductance(
        mine[3] - other[3],
        thick_ref[pl.ds(start - 1, 1)],
        thick_ref[pl.ds(start, 1)],
        wet_ref[...] > start,
    )
    rate = rate / (1.0 + rate * (mine[0] + other[0]))
    in_forward = rate * (other[1] - mine[1])
    in_adjoint = rate * (other[2] - mine[2])
    message_ref[:rows] = mine[4] + other[4] + in_adjoint * (mine[5] - other[5])
    if message_ref.shape[0] > rows + 8:
        message_ref[rows + 8 :] = damping_ref[...]
    even = lax.rem(place, 2) == 0
    pair = []
    for into, index in ((in_forward, 0), (in_adjoint, 1)):
        top = jnp.where(upper, 0.0, into)
        bottom = jnp.where(upper, into, 0.0)
        for step in range(len(sizes) - 2, -1, -1):
            flux_ref = flux_refs[step]
            flux = flux_ref[index] + top * flux_ref[2] + bottom * flux_ref[3]
            if step == 0:
                pair = [(top, flux), (-flux, bottom)]
            above = lax.rem(place // sizes[step], 2) == 0
            top, bottom = jnp.where(above, top, -flux), jnp.where(above, flux, bottom)
        ends_ref[2 * index] = top
        ends_ref[2 * index + 1] = bottom
    (top_above, bottom_above), (top_below, bottom_below) = pair
    top = jnp.where(even, top_below, top_above)
    bottom = jnp.where(even, bottom_below, bottom_above)
    mixed = edges_ref[:8] + edges_ref[8:16] * fold_surface(top) + edges_ref[16:] * fold_surface(bottom)
    weight = jnp.where(even, weight_ref[8:], weight_ref[:8])
    message_ref[rows : rows + 8] = weight * mixed


def rest_kernel(
    thick_ref, wet_ref, ends_ref, forward_ref, adjoint_ref, top_ref, bottom_ref, zonal_ref, merid_ref, factor_ref,
    from_west_ref, from_east_ref, next_tracer_ref, inner_ref, beside_ref,
):
    own, rows, width = forward_ref.shape
    first = lax.axis_index("lev") * own
    lane = lanes(rows, width)
    wet_levels = wet_ref[...]
    ends = [ends_ref[i] for i in range(4)]
    factor = factor_ref[...]
    beside_ref[0] = damping_of(from_west_ref[16:], thick_ref)
    beside_ref[1] = damping_of(from_east_ref[16:], thick_ref)
    for k in range(own):
        next_tracer_ref[k] = forward_ref[k] + top_ref[k] * ends[0] + bottom_ref[k] * ends[1]
        mixed = adjoint_ref[k] + top_ref[k] * ends[2] + bottom_ref[k] * ends[3]
        pulled = jnp.where(wet_levels > first + k, thick_ref[pl.ds(first + k, 1)] * mixed, 0.0)
        b_west = jnp.where(lane == 0, 0.0, turn(pulled, 1, 1))
        b_east = jnp.where(lane == width - 1, 0.0, turn(pulled, -1, 1))
        zonal = HALF_STEP * zonal_ref[k]
        u_next = jnp.where(lane == width - 1, spread_edges(factor, rows, k), turn(zonal, -1, 1))
        across = zonal * (pulled - b_west) + u_next * (b_east - pulled)
        step = HALF_STEP * merid_ref[k] * (pulled - turn(pulled, 1, 0))
        inner_ref[k] = pulled + across + step + turn(step, -1, 0)


def total(field):
    while field.ndim > 2:
        field = jnp.sum(field, axis=0)
    return jnp.sum(jnp.sum(field, axis=0, keepdims=True), axis=1, keepdims=True)


def routes(count):
    if count == 4:
        return [[1, 3, 0, 2], [3, 2, 1, 0], [2, 0, 3, 1]]
    return [[i ^ away for i in range(count)] for away in range(1, count)]


def crossed(route, lev_count):
    return [(s * lev_count + l, t * lev_count + (l ^ 1)) for s, t in enumerate(route) for l in range(lev_count)]


def owner_of(route, place):
    owner = 0
    for source, target in enumerate(route):
        owner = jnp.where(place == target, source, owner)
    return owner


def surface_kernel(
    gathered_ref, damping_ref, beside_ref, far_ref, inner_ref, factor_ref, tracer_adjoint_ref, surface_ref,
    source_scr, damping_scr, edges_scr,
):
    own, rows, width = inner_ref.shape
    count = gathered_ref.shape[0]
    place = lax.axis_index("sub")
    ways = [list(range(count))] + routes(count)[::-1]
    for i, route in enumerate(ways):
        owner = owner_of(route, place)
        source_scr[owner] = gathered_ref[i, :rows]
        if gathered_ref.shape[1] > rows + 8:
            damping_scr[owner] = gathered_ref[i, rows + 8 :]
        edges_scr[owner] = gathered_ref[i, rows : rows + 8]
    if gathered_ref.shape[1] == rows + 8:
        for away, field in ((0, damping_ref[...]), (3, beside_ref[0]), (1, beside_ref[1]), (2, far_ref[...])):
            damping_scr[lax.rem(place + away, count)] = field
    west_edges = edges_scr[lax.rem(place + count - 1, count)]
    east_edges = edges_scr[lax.rem(place + 1, count)]
    beside = factor_ref[...] * beside_edges(west_edges, east_edges)
    lane = lanes(rows, width)
    at_edge = jnp.logical_or(lane == 0, lane == width - 1)
    for k in range(own):
        tracer_adjoint_ref[k] = inner_ref[k] + jnp.where(at_edge, spread_edges(beside, rows, k), 0.0)

    first_lane = lax.broadcasted_iota(jnp.int32, (count, rows, width), 2) == 0
    last_lane = lax.broadcasted_iota(jnp.int32, (count, rows, width), 2) == width - 1
    damping = 4.0 + damping_scr[...]

    def passed(field, shift):
        return jnp.concatenate([field[-shift:], field[:-shift]]) if count > 1 else field

    def image_of(field):
        west = turn(field, 1, 2)
        west = jnp.where(first_lane, passed(west, 1), west)
        east = turn(field, -1, 2)
        east = jnp.where(last_lane, passed(east, -1), east)
        return damping * field - (west + east + turn(field, 1, 1) + turn(field, -1, 1))

    residual = source_scr[...]
    image = image_of(residual)
    norm = total(residual * residual)
    step_size = norm / total(residual * image)
    direction, along = residual, image
    surface = jnp.zeros_like(residual)
    for sweep in range(ITERS):
        surface = surface + step_size * direction
        if sweep + 1 < ITERS:
            residual = residual - step_size * along
            image = image_of(residual)
            norm_next = total(residual * residual)
            product = total(residual * image)
            growth = norm_next / norm
            step_size = norm_next / (product - growth * norm_next / step_size)
            direction = residual + growth * direction
            along = image + growth * along
            norm = norm_next
    source_scr[...] = surface
    surface_ref[...] = source_scr[place]


def on_device(tracer, zonal_flow, meridional_flow, cotangent, thickness, wet_levels):
    own, rows, width = tracer.shape
    lev_count = lax.axis_size("lev")
    sub_count = lax.axis_size("sub")
    edge = in_vmem(rows, width)
    levels = in_vmem(own, rows, width)
    message_rows = in_vmem(16 + rows, width)
    marks = pltpu.VMEM((rows, width), jnp.int32)
    thickness = pltpu.with_memory_space_constraint(thickness, pltpu.SMEM)

    tracer, zonal_flow, wet_levels, east, west, edges = pl.pallas_call(
        pack_kernel,
        out_shape=(levels, levels, marks, message_rows, message_rows, message_rows),
        in_specs=[pl.BlockSpec(memory_space=pl.ANY)] * 3,
        out_specs=(VMEM_IN,) * 6,
        scratch_shapes=[pltpu.SemaphoreType.DMA((3,))],
        name="pack",
    )(tracer, zonal_flow, wet_levels)
    ring = [(i, (i + 1) % sub_count) for i in range(sub_count)]
    from_west = lax.ppermute(east, "sub", ring)
    from_east = lax.ppermute(west, "sub", [(b, a) for a, b in ring])
    thickness, damping, weights, inside = pl.pallas_call(
        functools.partial(prepare_kernel, own),
        out_shape=(in_vmem(thickness.shape[0], width), edge, in_vmem(16, width), levels),
        in_specs=[SMEM_IN] + [VMEM_IN] * 4,
        out_specs=(VMEM_IN,) * 4,
        name="prepare",
    )(thickness, *near(wet_levels, tracer, zonal_flow, meridional_flow))

    block, forward, adjoint, top, bottom, factor = pl.pallas_call(
        local_kernel,
        out_shape=(in_vmem(N_BLOCK * rows, width), levels, levels, levels, levels, in_vmem(8, width)),
        in_specs=[VMEM_IN] * 8,
        out_specs=(VMEM_IN,) * 6,
        name="local",
    )(*near(thickness, wet_levels, weights, inside, cotangent, edges, from_west, from_east))
    edges = pl.pallas_call(
        edges_kernel, out_shape=in_vmem(24, width), in_specs=[VMEM_IN] * 3, out_specs=VMEM_IN, name="edges"
    )(*near(adjoint, top, bottom))
    other_edges = lax.ppermute(edges, "lev", [(i, i ^ 1) for i in range(lev_count)])

    sizes = [1]
    while sizes[-1] * 2 < lev_count:
        sizes.append(sizes[-1] * 2)
    fluxes = []
    for size in sizes:
        other = lax.ppermute(block, "lev", [(i, i ^ (2 * size - 1)) for i in range(lev_count)])
        if size == sizes[-1]:
            break
        if size == 1:
            other, other_edges = lax.optimization_barrier((other, other_edges))
        final = size * 2 == sizes[-1]
        block, flux = pl.pallas_call(
            functools.partial(merge_kernel, size, final, own),
            out_shape=(in_vmem((N_LAST if final else N_BLOCK) * rows, width), in_vmem(4, rows, width)),
            in_specs=[VMEM_IN] * 4,
            out_specs=(VMEM_IN,) * 2,
            name="merge",
        )(*near(thickness, wet_levels, block, other))
        fluxes.append(flux)

    lean = sub_count == 4
    far = damping
    if lean:
        _, far = lax.optimization_barrier((edges, damping))
        far = lax.ppermute(far, ("sub", "lev"), crossed([i ^ 2 for i in range(sub_count)], lev_count))
    message, ends = pl.pallas_call(
        functools.partial(final_kernel, sizes, own),
        out_shape=(in_vmem((rows if lean else 2 * rows) + 8, width), in_vmem(4, rows, width)),
        in_specs=[VMEM_IN] * (7 + len(fluxes)),
        out_specs=(VMEM_IN,) * 2,
        name="final",
    )(*near(thickness, wet_levels, weights, block, other, other_edges, damping, *fluxes))

    ways = routes(sub_count)[::-1]
    last = message
    if lean:
        last, far = lax.optimization_barrier((message, far))
    gathered = jnp.stack(
        [message]
        + [
            lax.ppermute(message if i else last, ("sub", "lev"), crossed(way, lev_count))
            for i, way in enumerate(ways)
        ]
    )

    next_tracer, inner, beside = pl.pallas_call(
        rest_kernel,
        out_shape=(jax.ShapeDtypeStruct(tracer.shape, jnp.float32), levels, in_vmem(2, rows, width)),
        in_specs=[VMEM_IN] * 12,
        out_specs=(VMEM_IN,) * 3,
        name="rest",
    )(
        *near(thickness, wet_levels, ends, forward, adjoint, top, bottom, zonal_flow, meridional_flow, factor),
        *near(from_west, from_east),
    )

    tracer_adjoint, surface = pl.pallas_call(
        surface_kernel,
        out_shape=(
            jax.ShapeDtypeStruct(tracer.shape, jnp.float32),
            jax.ShapeDtypeStruct((rows, width), jnp.float32),
        ),
        in_specs=[VMEM_IN] * 6,
        out_specs=(VMEM_IN,) * 2,
        scratch_shapes=[pltpu.VMEM((sub_count, rows, width), jnp.float32)] * 2
        + [pltpu.VMEM((sub_count, 8, width), jnp.float32)],
        name="surface",
    )(*near(gathered, damping, beside, far, inner, factor))
    return (next_tracer, tracer_adjoint, surface)


def solution(mesh):
    whole = P(("members", "lev"), None, "sub")
    return jax.shard_map(
        on_device,
        mesh=mesh,
        in_specs=(whole, whole, whole, whole, P(), P(None, "sub")),
        out_specs=(whole, whole, P("members", "sub")),
        check_vma=False,
    )
```

```python
import functools

import jax
import jax.numpy as jnp
from jax import lax
from jax.experimental import pallas as pl
from jax.experimental.pallas import tpu as pltpu
from jax.sharding import PartitionSpec as P

ITERS = 3
ADVECT_STEP = 0.25
MIX_RATE = 2.0
HALF_STEP = 0.5 * ADVECT_STEP

N_BLOCK = 12
N_LAST = 6

VMEM_IN = pl.BlockSpec(memory_space=pltpu.VMEM)
SMEM_IN = pl.BlockSpec(memory_space=pltpu.SMEM)


def in_vmem(*shape):
    return pltpu.VMEM(shape, jnp.float32)


def near(*arrays):
    return [pltpu.with_memory_space_constraint(array, pltpu.VMEM) for array in arrays]


def lanes(rows, width):
    return lax.broadcasted_iota(jnp.int32, (rows, width), 1)


def turn(field, shift, axis):
    size = field.shape[axis]
    shift = shift % size
    return field if shift == 0 else pltpu.roll(field, shift, axis)


def splat(scalar, width):
    return jnp.full((1, width), scalar, jnp.float32)


def conductance(drop, upper_thick, lower_thick, wet):
    spacing = 0.5 * (upper_thick + lower_thick)
    rate = 0.2 / spacing + spacing / (spacing * spacing + drop * drop)
    return jnp.where(wet, MIX_RATE * rate, 0.0)


def parity(width):
    return lax.rem(lanes(8, width), 2)


def fold_edges(levels):
    rows, width = levels[0].shape
    groups = rows // 8
    slot = width // groups
    pair = lanes(8, width) // 2
    folded = jnp.zeros((8, width), levels[0].dtype)
    for k, field in enumerate(levels):
        for group in range(groups):
            place = slot * group + 2 * k
            turned = turn(field[8 * group : 8 * group + 8], place + 1, 1)
            folded = jnp.where(pair == place // 2, turned, folded)
    return folded


def fold_surface(field):
    rows, width = field.shape
    groups = rows // 8
    slot = width // groups
    group_of = lanes(8, width) // slot
    folded = jnp.zeros((8, width), field.dtype)
    for group in range(groups):
        part = field[8 * group : 8 * group + 8]
        ends = jnp.where(
            parity(width) == 0,
            jnp.broadcast_to(part[:, width - 1 :], part.shape),
            jnp.broadcast_to(part[:, :1], part.shape),
        )
        folded = jnp.where(group_of == group, ends, folded)
    return folded


def beside_edges(from_west, from_east):
    return jnp.where(parity(from_west.shape[1]) == 0, turn(from_east, -1, 1), turn(from_west, 1, 1))


def spread_edges(beside, rows, k):
    width = beside.shape[1]
    groups = rows // 8
    slot = width // groups
    return jnp.concatenate([turn(beside, -(slot * group + 2 * k + 1), 1) for group in range(groups)])


def pack_kernel(
    tracer_hbm, zonal_hbm, wet_hbm, tracer_ref, zonal_ref, wet_ref, east_ref, west_ref, edges_ref, sems
):
    own = tracer_ref.shape[0]
    copies = [
        pltpu.make_async_copy(source, target, sems.at[i])
        for i, (source, target) in enumerate(
            ((tracer_hbm, tracer_ref), (zonal_hbm, zonal_ref), (wet_hbm, wet_ref))
        )
    ]
    for copy in copies:
        copy.start()
    copies[0].wait()
    east = fold_edges([tracer_ref[k] for k in range(own)])
    copies[1].wait()
    zonal = fold_edges([zonal_ref[k] for k in range(own)])
    copies[2].wait()
    for ref in (east_ref, west_ref, edges_ref):
        ref[:8] = east
        ref[8:16] = zonal
    east_ref[16:] = wet_ref[...].astype(jnp.float32)


def damping_of(wet_levels, thick_ref):
    level_count = thick_ref.shape[0]
    depth = jnp.zeros(wet_levels.shape, jnp.float32)
    for k in range(level_count):
        depth = depth + jnp.where(wet_levels > k, thick_ref[k : k + 1], 0.0)
    return 0.3 + depth / level_count


def prepare_kernel(
    own, thick_ref, wet_ref, tracer_ref, zonal_ref, merid_ref, rows_ref, damping_ref, weight_ref, inside_ref
):
    level_count = thick_ref.shape[0]
    rows, width = wet_ref.shape
    wet_levels = wet_ref[...]
    for k in range(level_count):
        rows_ref[k : k + 1] = splat(thick_ref[k], width)
    damping_ref[...] = damping_of(wet_levels, rows_ref)
    wet_edges = fold_surface(wet_levels)
    offset = lax.rem(lanes(8, width), width // (rows // 8)) // 2
    place = lax.axis_index("lev")
    for i in range(2):
        first = (place // 2 * 2 + i) * own
        thick = jnp.zeros((8, width), jnp.float32)
        for k in range(own):
            thick = jnp.where(offset == k, thick_ref[first + k], thick)
        weight_ref[8 * i : 8 * i + 8] = jnp.where(wet_edges > offset + first, thick, 0.0)
    first = place * own
    lane = lanes(rows, width)
    for k in range(own):
        values = tracer_ref[k]
        zonal = zonal_ref[k]
        c_west = jnp.where(lane == 0, 0.0, turn(values, 1, 1))
        u_next = jnp.where(lane == width - 1, 0.0, turn(zonal, -1, 1))
        flux_y = merid_ref[k] * (turn(values, 1, 0) + values)
        change = u_next * (values + turn(values, -1, 1)) - zonal * (c_west + values) + (turn(flux_y, -1, 0) - flux_y)
        inside_ref[k] = jnp.where(wet_levels > first + k, values - HALF_STEP * change, 0.0)


def local_kernel(
    thick_ref, wet_ref, weight_ref, inside_ref, cot_ref, edges_ref, from_west_ref, from_east_ref,
    block_ref, forward_ref, adjoint_ref, top_ref, bottom_ref, factor_ref,
):
    own, rows, width = cot_ref.shape
    first = lax.axis_index("lev") * own
    lane = lanes(rows, width)
    at_edge = jnp.logical_or(lane == 0, lane == width - 1)
    even = parity(width) == 0
    wet_levels = wet_ref[...]
    factor = HALF_STEP * jnp.where(even, turn(from_east_ref[8:16], -1, 1), -edges_ref[8:16])
    factor_ref[...] = factor
    beside = beside_edges(from_west_ref[:8], from_east_ref[:8])
    beside = -factor * jnp.where(even, edges_ref[:8] + beside, beside)
    weight = jnp.where(lax.rem(lax.axis_index("lev"), 2) == 0, weight_ref[:8], weight_ref[8:])
    beside = jnp.where(weight > 0.0, beside, 0.0)
    forward = []
    for k in range(own):
        forward.append(inside_ref[k] + jnp.where(at_edge, spread_edges(beside, rows, k), 0.0))

    thick = [thick_ref[pl.ds(first + k, 1)] for k in range(own)]
    conduct = [None]
    for k in range(1, own):
        conduct.append(
            conductance(forward[k] - forward[k - 1], thick[k - 1], thick[k], wet_levels > first + k)
        )
    pivot = jnp.broadcast_to(thick[0], (rows, width))
    ratio, scale = [None], []
    g_forward = [thick[0] * forward[0]]
    g_adjoint = [cot_ref[0]]
    g_top = [jnp.ones((rows, width), jnp.float32)]
    for k in range(1, own):
        inverse = 1.0 / (pivot + conduct[k])
        scale.append(inverse)
        ratio.append(conduct[k] * inverse)
        pivot = thick[k] + pivot * ratio[k]
        g_forward.append(thick[k] * forward[k] + ratio[k] * g_forward[k - 1])
        g_adjoint.append(cot_ref[k] + ratio[k] * g_adjoint[k - 1])
        g_top.append(ratio[k] * g_top[k - 1])
    scale.append(1.0 / pivot)

    def put(index, field):
        block_ref[rows * index : rows * (index + 1)] = field

    last = own - 1
    y_forward = g_forward[last] * scale[last]
    y_adjoint = g_adjoint[last] * scale[last]
    y_top = g_top[last] * scale[last]
    y_bottom = scale[last]
    put(1, y_top)
    put(2, y_bottom)
    put(4, y_forward)
    put(6, y_adjoint)
    put(7, forward[0])
    put(8, forward[last])
    sums = [jnp.zeros((rows, width), jnp.float32)] * 3
    for k in range(last, -1, -1):
        if k < last:
            y_forward = g_forward[k] * scale[k] + ratio[k + 1] * y_forward
            y_adjoint = g_adjoint[k] * scale[k] + ratio[k + 1] * y_adjoint
            y_top = g_top[k] * scale[k] + ratio[k + 1] * y_top
            y_bottom = ratio[k + 1] * y_bottom
        forward_ref[k] = y_forward
        adjoint_ref[k] = y_adjoint
        top_ref[k] = y_top
        bottom_ref[k] = y_bottom
        square = thick[k] * thick[k]
        sums = [s + square * y for s, y in zip(sums, (y_adjoint, y_top, y_bottom))]
    put(0, y_top)
    put(3, y_forward)
    put(5, y_adjoint)
    for i in range(3):
        put(9 + i, sums[i])


def edges_kernel(adjoint_ref, top_ref, bottom_ref, wet_ref, from_west_ref, edges_ref, wet_pair_ref):
    for i, ref in enumerate((adjoint_ref, top_ref, bottom_ref)):
        edges_ref[8 * i : 8 * i + 8] = fold_edges([ref[k] for k in range(ref.shape[0])])
    wet_pair_ref[0] = wet_ref[...].astype(jnp.float32)
    wet_pair_ref[1] = from_west_ref[16:]


def merge_kernel(size, final, own, thick_ref, wet_ref, mine_ref, other_ref, block_ref, flux_ref):
    place = lax.axis_index("lev")
    rows, width = wet_ref.shape
    upper = lax.rem(place // size, 2) == 0
    mine = [mine_ref[rows * i : rows * (i + 1)] for i in range(N_BLOCK)]
    other = [other_ref[rows * i : rows * (i + 1)] for i in range(N_BLOCK)]
    above = [jnp.where(upper, a, b) for a, b in zip(mine, other)]
    below = [jnp.where(upper, b, a) for a, b in zip(mine, other)]
    start = (place // (2 * size) * 2 + 1) * size * own
    rate = conductance(
        below[7] - above[8],
        thick_ref[pl.ds(start - 1, 1)],
        thick_ref[pl.ds(start, 1)],
        wet_ref[...] > start,
    )
    rate = rate / (1.0 + rate * (below[0] + above[2]))
    by_forward = rate * (below[3] - above[4])
    by_adjoint = rate * (below[5] - above[6])
    by_top = -rate * above[1]
    by_bottom = rate * below[1]
    flux_ref[0] = by_forward
    flux_ref[1] = by_adjoint
    flux_ref[2] = by_top
    flux_ref[3] = by_bottom
    spread = above[11] - below[10]
    merged = [
        above[0] + above[1] * by_top,
        -below[1] * by_top,
        below[2] - below[1] * by_bottom,
        above[3] + above[1] * by_forward,
        below[4] - below[1] * by_forward,
        above[5] + above[1] * by_adjoint,
        below[6] - below[1] * by_adjoint,
        above[7],
        below[8],
        above[9] + below[9] + by_adjoint * spread,
        above[10] + by_top * spread,
        below[11] + by_bottom * spread,
    ]
    if final:
        upper_next = lax.rem(place // (2 * size), 2) == 0
        merged = last_fields(upper_next, merged)
    for i, field in enumerate(merged):
        block_ref[rows * i : rows * (i + 1)] = field


def last_fields(upper, block):
    return [
        jnp.where(upper, block[2], block[0]),
        jnp.where(upper, block[4], block[3]),
        jnp.where(upper, block[6], block[5]),
        jnp.where(upper, block[8], block[7]),
        block[9],
        jnp.where(upper, block[11], block[10]),
    ]


def final_kernel(
    sizes, own, thick_ref, wet_ref, weight_ref, mine_ref, other_ref, edges_ref, damping_ref, *rest
):
    flux_refs, message_ref, ends_ref = rest[:-2], rest[-2], rest[-1]
    rows, width = wet_ref.shape
    place = lax.axis_index("lev")
    size = sizes[-1]
    upper = lax.rem(place // size, 2) == 0
    start = (place // (2 * size) * 2 + 1) * size * own
    mine = [mine_ref[rows * i : rows * (i + 1)] for i in range(N_LAST)]
    other = [other_ref[rows * i : rows * (i + 1)] for i in range(N_LAST)]
    rate = conductance(
        mine[3] - other[3],
        thick_ref[pl.ds(start - 1, 1)],
        thick_ref[pl.ds(start, 1)],
        wet_ref[...] > start,
    )
    rate = rate / (1.0 + rate * (mine[0] + other[0]))
    in_forward = rate * (other[1] - mine[1])
    in_adjoint = rate * (other[2] - mine[2])
    message_ref[:rows] = mine[4] + other[4] + in_adjoint * (mine[5] - other[5])
    if message_ref.shape[0] > rows + 8:
        message_ref[rows + 8 :] = damping_ref[...]
    even = lax.rem(place, 2) == 0
    pair = []
    for into, index in ((in_forward, 0), (in_adjoint, 1)):
        top = jnp.where(upper, 0.0, into)
        bottom = jnp.where(upper, into, 0.0)
        for step in range(len(sizes) - 2, -1, -1):
            flux_ref = flux_refs[step]
            flux = flux_ref[index] + top * flux_ref[2] + bottom * flux_ref[3]
            if step == 0:
                pair = [(top, flux), (-flux, bottom)]
            above = lax.rem(place // sizes[step], 2) == 0
            top, bottom = jnp.where(above, top, -flux), jnp.where(above, flux, bottom)
        ends_ref[2 * index] = top
        ends_ref[2 * index + 1] = bottom
    (top_above, bottom_above), (top_below, bottom_below) = pair
    top = jnp.where(even, top_below, top_above)
    bottom = jnp.where(even, bottom_below, bottom_above)
    mixed = edges_ref[:8] + edges_ref[8:16] * fold_surface(top) + edges_ref[16:] * fold_surface(bottom)
    weight = jnp.where(even, weight_ref[8:], weight_ref[:8])
    message_ref[rows : rows + 8] = weight * mixed


def rest_kernel(
    thick_ref, wet_ref, ends_ref, forward_ref, adjoint_ref, top_ref, bottom_ref, zonal_ref, merid_ref, factor_ref,
    wet_pair_ref, far_ref, next_tracer_ref, inner_ref, dampings_ref,
):
    own, rows, width = forward_ref.shape
    first = lax.axis_index("lev") * own
    lane = lanes(rows, width)
    wet_levels = wet_ref[...]
    ends = [ends_ref[i] for i in range(4)]
    factor = factor_ref[...]
    for i, wet_levels_there in enumerate((wet_pair_ref[1], far_ref[1], far_ref[0])):
        dampings_ref[i] = damping_of(wet_levels_there, thick_ref)
    for k in range(own):
        next_tracer_ref[k] = forward_ref[k] + top_ref[k] * ends[0] + bottom_ref[k] * ends[1]
        mixed = adjoint_ref[k] + top_ref[k] * ends[2] + bottom_ref[k] * ends[3]
        pulled = jnp.where(wet_levels > first + k, thick_ref[pl.ds(first + k, 1)] * mixed, 0.0)
        b_west = jnp.where(lane == 0, 0.0, turn(pulled, 1, 1))
        b_east = jnp.where(lane == width - 1, 0.0, turn(pulled, -1, 1))
        zonal = HALF_STEP * zonal_ref[k]
        u_next = jnp.where(lane == width - 1, spread_edges(factor, rows, k), turn(zonal, -1, 1))
        across = zonal * (pulled - b_west) + u_next * (b_east - pulled)
        step = HALF_STEP * merid_ref[k] * (pulled - turn(pulled, 1, 0))
        inner_ref[k] = pulled + across + step + turn(step, -1, 0)


def total(field):
    while field.ndim > 2:
        field = jnp.sum(field, axis=0)
    return jnp.sum(jnp.sum(field, axis=0, keepdims=True), axis=1, keepdims=True)


def routes(count):
    if count == 4:
        return [[1, 3, 0, 2], [3, 2, 1, 0], [2, 0, 3, 1]]
    return [[i ^ away for i in range(count)] for away in range(1, count)]


def crossed(route, lev_count):
    return [(s * lev_count + l, t * lev_count + (l ^ 1)) for s, t in enumerate(route) for l in range(lev_count)]


def owner_of(route, place):
    owner = 0
    for source, target in enumerate(route):
        owner = jnp.where(place == target, source, owner)
    return owner


def surface_kernel(
    gathered_ref, damping_ref, dampings_ref, inner_ref, factor_ref, tracer_adjoint_ref, surface_ref,
    source_scr, damping_scr, edges_scr,
):
    own, rows, width = inner_ref.shape
    count = gathered_ref.shape[0]
    place = lax.axis_index("sub")
    ways = [list(range(count))] + routes(count)[::-1]
    for i, route in enumerate(ways):
        owner = owner_of(route, place)
        source_scr[owner] = gathered_ref[i, :rows]
        if gathered_ref.shape[1] > rows + 8:
            damping_scr[owner] = gathered_ref[i, rows + 8 :]
        edges_scr[owner] = gathered_ref[i, rows : rows + 8]
    if gathered_ref.shape[1] == rows + 8:
        for away, field in ((0, damping_ref[...]), (3, dampings_ref[0]), (1, dampings_ref[1]), (2, dampings_ref[2])):
            damping_scr[lax.rem(place + away, count)] = field
    west_edges = edges_scr[lax.rem(place + count - 1, count)]
    east_edges = edges_scr[lax.rem(place + 1, count)]
    beside = factor_ref[...] * beside_edges(west_edges, east_edges)
    lane = lanes(rows, width)
    at_edge = jnp.logical_or(lane == 0, lane == width - 1)
    for k in range(own):
        tracer_adjoint_ref[k] = inner_ref[k] + jnp.where(at_edge, spread_edges(beside, rows, k), 0.0)

    first_lane = lax.broadcasted_iota(jnp.int32, (count, rows, width), 2) == 0
    last_lane = lax.broadcasted_iota(jnp.int32, (count, rows, width), 2) == width - 1
    damping = 4.0 + damping_scr[...]

    def passed(field, shift):
        return jnp.concatenate([field[-shift:], field[:-shift]]) if count > 1 else field

    def image_of(field):
        west = turn(field, 1, 2)
        west = jnp.where(first_lane, passed(west, 1), west)
        east = turn(field, -1, 2)
        east = jnp.where(last_lane, passed(east, -1), east)
        return damping * field - (west + east + turn(field, 1, 1) + turn(field, -1, 1))

    residual = source_scr[...]
    image = image_of(residual)
    norm = total(residual * residual)
    step_size = norm / total(residual * image)
    direction, along = residual, image
    surface = jnp.zeros_like(residual)
    for sweep in range(ITERS):
        surface = surface + step_size * direction
        if sweep + 1 < ITERS:
            residual = residual - step_size * along
            image = image_of(residual)
            norm_next = total(residual * residual)
            product = total(residual * image)
            growth = norm_next / norm
            step_size = norm_next / (product - growth * norm_next / step_size)
            direction = residual + growth * direction
            along = image + growth * along
            norm = norm_next
    source_scr[...] = surface
    surface_ref[...] = source_scr[place]


def on_device(tracer, zonal_flow, meridional_flow, cotangent, thickness, wet_levels):
    own, rows, width = tracer.shape
    lev_count = lax.axis_size("lev")
    sub_count = lax.axis_size("sub")
    edge = in_vmem(rows, width)
    levels = in_vmem(own, rows, width)
    marks = pltpu.VMEM((rows, width), jnp.int32)
    thickness = pltpu.with_memory_space_constraint(thickness, pltpu.SMEM)

    tracer, zonal_flow, wet_levels, east, west, edges = pl.pallas_call(
        pack_kernel,
        out_shape=(levels, levels, marks, in_vmem(16 + rows, width), in_vmem(16, width), in_vmem(16, width)),
        in_specs=[pl.BlockSpec(memory_space=pl.ANY)] * 3,
        out_specs=(VMEM_IN,) * 6,
        scratch_shapes=[pltpu.SemaphoreType.DMA((3,))],
        name="pack",
    )(tracer, zonal_flow, wet_levels)
    ring = [(i, (i + 1) % sub_count) for i in range(sub_count)]
    from_west = lax.ppermute(east, "sub", ring)
    from_east = lax.ppermute(west, "sub", [(b, a) for a, b in ring])
    thickness, damping, weights, inside = pl.pallas_call(
        functools.partial(prepare_kernel, own),
        out_shape=(in_vmem(thickness.shape[0], width), edge, in_vmem(16, width), levels),
        in_specs=[SMEM_IN] + [VMEM_IN] * 4,
        out_specs=(VMEM_IN,) * 4,
        name="prepare",
    )(thickness, *near(wet_levels, tracer, zonal_flow, meridional_flow))

    block, forward, adjoint, top, bottom, factor = pl.pallas_call(
        local_kernel,
        out_shape=(in_vmem(N_BLOCK * rows, width), levels, levels, levels, levels, in_vmem(8, width)),
        in_specs=[VMEM_IN] * 8,
        out_specs=(VMEM_IN,) * 6,
        name="local",
    )(*near(thickness, wet_levels, weights, inside, cotangent, edges, from_west, from_east))
    edges, wet_pair = pl.pallas_call(
        edges_kernel,
        out_shape=(in_vmem(24, width), in_vmem(2, rows, width)),
        in_specs=[VMEM_IN] * 5,
        out_specs=(VMEM_IN,) * 2,
        name="edges",
    )(*near(adjoint, top, bottom, wet_levels, from_west))
    other_edges = lax.ppermute(edges, "lev", [(i, i ^ 1) for i in range(lev_count)])

    sizes = [1]
    while sizes[-1] * 2 < lev_count:
        sizes.append(sizes[-1] * 2)
    fluxes = []
    for size in sizes:
        other = lax.ppermute(block, "lev", [(i, i ^ (2 * size - 1)) for i in range(lev_count)])
        if size == sizes[-1]:
            break
        if size == 1:
            other, other_edges = lax.optimization_barrier((other, other_edges))
        final = size * 2 == sizes[-1]
        block, flux = pl.pallas_call(
            functools.partial(merge_kernel, size, final, own),
            out_shape=(in_vmem((N_LAST if final else N_BLOCK) * rows, width), in_vmem(4, rows, width)),
            in_specs=[VMEM_IN] * 4,
            out_specs=(VMEM_IN,) * 2,
            name="merge",
        )(*near(thickness, wet_levels, block, other))
        fluxes.append(flux)

    lean = sub_count == 4
    far = wet_pair
    if lean:
        _, far = lax.optimization_barrier((edges, far))
        far = lax.ppermute(far, ("sub", "lev"), crossed([i ^ 2 for i in range(sub_count)], lev_count))
    message, ends = pl.pallas_call(
        functools.partial(final_kernel, sizes, own),
        out_shape=(in_vmem((rows if lean else 2 * rows) + 8, width), in_vmem(4, rows, width)),
        in_specs=[VMEM_IN] * (7 + len(fluxes)),
        out_specs=(VMEM_IN,) * 2,
        name="final",
    )(*near(thickness, wet_levels, weights, block, other, other_edges, damping, *fluxes))

    ways = routes(sub_count)[::-1]
    last = message
    if lean:
        last, far = lax.optimization_barrier((message, far))
    gathered = jnp.stack(
        [message]
        + [
            lax.ppermute(message if i else last, ("sub", "lev"), crossed(way, lev_count))
            for i, way in enumerate(ways)
        ]
    )

    next_tracer, inner, dampings = pl.pallas_call(
        rest_kernel,
        out_shape=(jax.ShapeDtypeStruct(tracer.shape, jnp.float32), levels, in_vmem(3, rows, width)),
        in_specs=[VMEM_IN] * 12,
        out_specs=(VMEM_IN,) * 3,
        name="rest",
    )(
        *near(thickness, wet_levels, ends, forward, adjoint, top, bottom, zonal_flow, meridional_flow, factor),
        *near(wet_pair, far),
    )

    tracer_adjoint, surface = pl.pallas_call(
        surface_kernel,
        out_shape=(
            jax.ShapeDtypeStruct(tracer.shape, jnp.float32),
            jax.ShapeDtypeStruct((rows, width), jnp.float32),
        ),
        in_specs=[VMEM_IN] * 5,
        out_specs=(VMEM_IN,) * 2,
        scratch_shapes=[pltpu.VMEM((sub_count, rows, width), jnp.float32)] * 2
        + [pltpu.VMEM((sub_count, 8, width), jnp.float32)],
        name="surface",
    )(*near(gathered, damping, dampings, inner, factor))
    return (next_tracer, tracer_adjoint, surface)


def solution(mesh):
    whole = P(("members", "lev"), None, "sub")
    return jax.shard_map(
        on_device,
        mesh=mesh,
        in_specs=(whole, whole, whole, whole, P(), P(None, "sub")),
        out_specs=(whole, whole, P("members", "sub")),
        check_vma=False,
    )
```
